512 devices in a mesh: gx: 16 (over z_lo, y), gy: 8 (over x, core), gz: 4 (over z_hi).
Axes of the slice: x: 4, y: 8, z: 8 (z_hi: 4, z_lo: 2; z = z_hi * 2 + z_lo), core: 2. Of those that a mesh axis runs over, the one named last changes fastest.
Arguments:
- offsets: bfloat16 [3, 48, 4096], replicated, may hold values from -0.14941406 to 0.14941406
- displacement: float32 [384, 3, 256, 512], P('gx', None, 'gy', 'gz'), may hold values from -0.25 to 0.25
- adjoint: float32 [384, 3, 256, 512], P('gx', None, 'gy', 'gz'), may hold values from -1.5 to 1.5
- span_x: int32 [384], replicated, may hold values from 0 to 44, never falling along the last dimension, each value on 1 to 18 neighbouring positions
- span_y: int32 [256], replicated, may hold values from 0 to 60, never falling along the last dimension, each value on 1 to 9 neighbouring positions
- span_z: int32 [512], replicated, may hold values from 0 to 60, never falling along the last dimension, each value on 1 to 17 neighbouring positions
Outputs:
- control_gradient: float32 [3, 48, 4096], replicated
The draws below stay inside these ranges and needn't reach their ends.
Inputs may be any that keep to these rules, and one draw needn't show every extreme that they name: span_x never falls along the node lines; each span 0 to 44 holds 1 to 18 node lines. span_y never falls; each span 0 to 60 holds 1 to 9 node lines. span_z never falls; each span 0 to 60 holds 1 to 17 node lines.
All inputs are finite; a program needn't handle non-finite values.
Results may differ from the reference program's by a relative error of at most 0.0003.
Values sent between devices are 32-bit elements; how exact they have to be, the bound alone decides.
No kernel may reach another device: no remote copies, remote signals or barrier semaphores. Data moves between devices by JAX's collectives and lax.ppermute only.
A program may use at most 128 MiB of HBM per device.

```python
import math
import jax
import jax.numpy as jnp
import numpy as np
from jax import lax

NCX = 48
NCY = 64
NCZ = 64
NX = 384
NY = 256
NZ = 512


def draw_displacement(key, part):
    key = jax.random.fold_in(key, 7)
    sign_key, size_key, phase_key, rough_key = jax.random.split(key, 4)
    wave_signs = jnp.where(jax.random.bernoulli(sign_key, 0.5, (3, 2, 3)), 1.0, -1.0)
    wave_vector = wave_signs * jax.random.uniform(size_key, (3, 2, 3), jnp.float32, 0.3, 0.75)
    wave_phase = jax.random.uniform(phase_key, (3, 2), jnp.float32, 0.0, 2.0 * math.pi)
    mode_share = jnp.array([0.12, 0.08], jnp.float32)
    amplitude = mode_share[None, :] / jnp.sum(jnp.abs(wave_vector), axis=-1)
    along_x = jnp.arange(NX, dtype=jnp.float32)[:, None, None]
    along_y = jnp.arange(NY, dtype=jnp.float32)[None, :, None]
    along_z = jnp.arange(NZ, dtype=jnp.float32)[None, None, :]
    components = []
    for component in range(3):
        component_field = jnp.zeros((NX, NY, NZ), jnp.float32)
        for mode_index in range(2):
            angle_field = wave_vector[component, mode_index, 0] * along_x + wave_vector[component, mode_index, 1] * along_y + wave_vector[component, mode_index, 2] * along_z + wave_phase[component, mode_index]
            component_field = component_field + amplitude[component, mode_index] * jnp.sin(angle_field)
        components.append(component_field)
    smooth_part = jnp.stack(components, axis=1)
    rough_part = jnp.clip(0.004 * jax.random.normal(rough_key, smooth_part.shape, jnp.float32), -0.012, 0.012)
    return smooth_part + rough_part


def level_of(own_key, shape, shards, smallest, top_value):
    gain = 1.0
    for axis_at, blocks in shards:
        draws = jax.random.uniform(jax.random.fold_in(jax.random.fold_in(own_key, 6), axis_at), (blocks,), jnp.float32, smallest / len(shards), top_value / len(shards))
        gain = gain * jnp.repeat(jnp.exp(draws), shape[axis_at] // blocks).reshape((-1,) + (1,) * (len(shape) - 1 - axis_at))
    return gain


def length_profile(count, total, reach, skew):
    weights = [(1 << 20) // math.isqrt(standing ** skew) + 1 for standing in range(2, count + 1)]
    spare, holding = total - reach - (count - 1), [1] * (count - 1)
    while spare > 0:
        free = [i for i in range(count - 1) if holding[i] < reach]
        mass, remaining = sum([weights[i] for i in free]), spare
        for i in free:
            extra = min(reach - holding[i], max(1, remaining * weights[i] // mass), spare)
            holding[i] = holding[i] + extra
            spare = spare - extra
    return np.array([reach] + holding)


def ragged_sizes(key, count, total, limit, slope):
    if count == 2:
        one = jax.random.randint(key, (), max(1, total - limit), min(limit, total - 1) + 1)
        return jnp.stack([one, total - one])
    tallies = jnp.asarray(length_profile(count, total, limit, slope), jnp.int32)
    couples = (count - 1) // 2
    giver, sink = tallies[1:1 + 2 * couples:2], tallies[2:2 + 2 * couples:2]
    room = jnp.minimum(giver - 1, limit - sink)
    shifted = jax.random.randint(jax.random.fold_in(key, 1), (couples,), 0, 1 << 20) % (room + 1)
    tallies = tallies.at[1:1 + 2 * couples:2].set(giver - shifted).at[2:2 + 2 * couples:2].set(sink + shifted)
    return tallies[jax.random.permutation(jax.random.fold_in(key, 2), count)]


def scatter_about(stream_key, dims, scale, reach, cuts=(), kind=jnp.bfloat16):
    entries = jax.random.normal(stream_key, dims, jnp.float32) * scale
    if len(cuts) > 0:
        entries = level_of(stream_key, dims, cuts, -0.22, 0.18) * entries
    return jnp.clip(entries, min=-reach, max=reach).astype(kind)


def setup_inputs(seed: int = 0) -> dict:
    streams_of = jax.random.split(jax.random.key(seed), 7)
    return {
        "offsets": jnp.clip(jax.random.uniform(streams_of[0], (3, NCX, NCY * NCZ), jnp.float32, -0.14941406, 0.14941406), -0.14941406, 0.14941406).astype(jnp.bfloat16),
        "displacement": draw_displacement(jax.random.fold_in(streams_of[6], 71), 0),
        "adjoint": scatter_about(streams_of[2], (NX, 3, NY, NZ), 0.1, 1.5, ((0, 16), (2, 8), (3, 4)), jnp.float32),
        "span_x": jnp.searchsorted(jnp.cumsum(ragged_sizes(streams_of[3], NCX - 3, NX, 2 * NX // (NCX - 3) + 1, 1)), jnp.arange(NX), side="right").astype(jnp.int32),
        "span_y": jnp.searchsorted(jnp.cumsum(ragged_sizes(streams_of[4], NCY - 3, NY, 2 * NY // (NCY - 3) + 1, 1)), jnp.arange(NY), side="right").astype(jnp.int32),
        "span_z": jnp.searchsorted(jnp.cumsum(ragged_sizes(streams_of[5], NCZ - 3, NZ, 2 * NZ // (NCZ - 3) + 1, 1)), jnp.arange(NZ), side="right").astype(jnp.int32),
    }


MU_SHEAR = 40.0
LAME_FIRST = 60.0
TAPER_RATE = 0.8
HIGHEST_PRECISION = lax.Precision.HIGHEST

def basis_matrix(span_table, first_row, row_count, col_count):
    all_rows = jnp.arange(span_table.shape[0], dtype=jnp.int32)
    own_rows = first_row + jnp.arange(row_count, dtype=jnp.int32)
    own_spans = lax.dynamic_slice_in_dim(span_table, first_row, row_count)
    matches = span_table[None, :] == own_spans[:, None]
    counted = lax.optimization_barrier(jnp.sum(matches.astype(jnp.float32), axis=1))
    earlier = lax.optimization_barrier(jnp.sum((matches & (all_rows[None, :] < own_rows[:, None])).astype(jnp.float32), axis=1))
    local_param = (earlier + 0.5) / counted
    complement = 1.0 - local_param
    square = local_param * local_param
    param_cube = square * local_param
    weights = [complement * complement * complement / 6.0, (3.0 * param_cube - 6.0 * square + 4.0) / 6.0, (-3.0 * param_cube + 3.0 * square + 3.0 * local_param + 1.0) / 6.0, param_cube / 6.0]
    columns = jnp.arange(col_count, dtype=jnp.int32)
    offset_table = columns[None, :] - own_spans[:, None]
    matrix = jnp.zeros((row_count, col_count), jnp.float32)
    for degree_term in range(4):
        matrix = matrix + jnp.where(offset_table == degree_term, weights[degree_term][:, None], 0.0)
    return matrix

def control_points(offsets, node_x, node_y, node_z):
    offset_grid = offsets.astype(jnp.float32).reshape(3, NCX, NCY, NCZ)
    along_x = jnp.arange(NCX, dtype=jnp.float32)[:, None, None]
    across_y = jnp.arange(NCY, dtype=jnp.float32)[None, :, None]
    through_z = jnp.arange(NCZ, dtype=jnp.float32)[None, None, :]
    step_x = 2.0 * node_x / (NCX - 3)
    step_y = 2.0 * node_y / (NCY - 3)
    step_z = 2.0 * node_z / (NCZ - 3)
    taper_scale = 1.0 + TAPER_RATE * along_x / (NCX - 1)
    coord_x = step_x * (along_x + offset_grid[0])
    coord_y = step_y * (taper_scale * (across_y - 0.5 * (NCY - 1)) + offset_grid[1])
    coord_z = step_z * (taper_scale * (through_z - 0.5 * (NCZ - 1)) + offset_grid[2])
    return jnp.stack([coord_x, coord_y, coord_z])

def node_positions(points, basis_x, basis_y, basis_z):
    partial_x = jnp.einsum('cabz,ia->icbz', points, basis_x, precision=HIGHEST_PRECISION)
    partial_y = jnp.einsum('icbz,jb->icjz', partial_x, basis_y, precision=HIGHEST_PRECISION)
    return jnp.einsum('icjz,kz->icjk', partial_y, basis_z, precision=HIGHEST_PRECISION)

def control_terms(node_grad, basis_x, basis_y, basis_z):
    along_z = jnp.einsum('icjk,kz->icjz', node_grad, basis_z, precision=HIGHEST_PRECISION)
    along_y = jnp.einsum('icjz,jb->icbz', along_z, basis_y, precision=HIGHEST_PRECISION)
    return jnp.einsum('icbz,ia->cabz', along_y, basis_x, precision=HIGHEST_PRECISION)

def derivatives(lower_values, upper_values):
    y_count = lower_values.shape[1] - 1
    z_count = lower_values.shape[2] - 1

    def corner(values, shift_y, shift_z):
        return values[shift_y:shift_y + y_count, shift_z:shift_z + z_count]
    result = []
    for component in range(lower_values.shape[0]):
        lower_field = lower_values[component]
        upper_field = upper_values[component]
        d_first = (corner(upper_field, 0, 0) + corner(upper_field, 0, 1) + corner(upper_field, 1, 0) + corner(upper_field, 1, 1) - corner(lower_field, 0, 0) - corner(lower_field, 0, 1) - corner(lower_field, 1, 0) - corner(lower_field, 1, 1)) * 0.125
        d_second = (corner(lower_field, 1, 0) + corner(lower_field, 1, 1) + corner(upper_field, 1, 0) + corner(upper_field, 1, 1) - corner(lower_field, 0, 0) - corner(lower_field, 0, 1) - corner(upper_field, 0, 0) - corner(upper_field, 0, 1)) * 0.125
        d_third = (corner(lower_field, 0, 1) + corner(lower_field, 1, 1) + corner(upper_field, 0, 1) + corner(upper_field, 1, 1) - corner(lower_field, 0, 0) - corner(lower_field, 1, 0) - corner(upper_field, 0, 0) - corner(upper_field, 1, 0)) * 0.125
        result.append([d_first, d_second, d_third])
    return result

def invert(matrix):

    def cofactor(row_index, col_index):
        keep_rows = [other for other in range(3) if other != row_index]
        keep_cols = [other for other in range(3) if other != col_index]
        minor_value = matrix[keep_rows[0]][keep_cols[0]] * matrix[keep_rows[1]][keep_cols[1]] - matrix[keep_rows[0]][keep_cols[1]] * matrix[keep_rows[1]][keep_cols[0]]
        return minor_value if (row_index + col_index) % 2 == 0 else -minor_value
    cofactors = [[cofactor(row_index, col_index) for col_index in range(3)] for row_index in range(3)]
    determinant = matrix[0][0] * cofactors[0][0] + matrix[0][1] * cofactors[0][1] + matrix[0][2] * cofactors[0][2]
    inverse = [[cofactors[col_index][row_index] / determinant for col_index in range(3)] for row_index in range(3)]
    return (determinant, inverse)

def product(left_matrix, right_matrix):
    return [[left_matrix[row_index][0] * right_matrix[0][col_index] + left_matrix[row_index][1] * right_matrix[1][col_index] + left_matrix[row_index][2] * right_matrix[2][col_index] for col_index in range(3)] for row_index in range(3)]

def layer_terms(lower_pos, upper_pos, lower_rest, upper_rest, live_mask, counted):
    jacobian = derivatives(lower_pos, upper_pos)
    disp_grad = derivatives(lower_rest[:3], upper_rest[:3])
    adj_grad = derivatives(lower_rest[3:], upper_rest[3:])
    jacobian = [[jnp.where(live_mask, jacobian[row_index][col_index], 1.0 if row_index == col_index else 0.0) for col_index in range(3)] for row_index in range(3)]
    disp_grad = [[jnp.where(live_mask, disp_grad[row_index][col_index], 0.0) for col_index in range(3)] for row_index in range(3)]
    adj_grad = [[jnp.where(live_mask, adj_grad[row_index][col_index], 0.0) for col_index in range(3)] for row_index in range(3)]
    det_ref, inv_ref = invert(jacobian)
    strain = product(disp_grad, inv_ref)
    virtual = product(adj_grad, inv_ref)
    deform = [[strain[row_index][col_index] + (1.0 if row_index == col_index else 0.0) for col_index in range(3)] for row_index in range(3)]
    det_def, inv_def = invert(deform)
    log_det = jnp.log(det_def)
    stretch = 0.0
    virtual_work = 0.0
    for row_index in range(3):
        for col_index in range(3):
            stretch = stretch + deform[row_index][col_index] * deform[row_index][col_index]
            stress = MU_SHEAR * (deform[row_index][col_index] - inv_def[col_index][row_index]) + LAME_FIRST * log_det * inv_def[col_index][row_index]
            virtual_work = virtual_work + stress * virtual[row_index][col_index]
    energy = 0.5 * MU_SHEAR * (stretch - 3.0 - 2.0 * log_det) + 0.5 * LAME_FIRST * log_det * log_det
    volume = 8.0 * det_ref
    lagrangian = jnp.sum(jnp.where(live_mask, volume * (energy - virtual_work), 0.0))
    total_volume = jnp.sum(jnp.where(counted, volume, 0.0))
    return (lagrangian, total_volume)

def layer_gradient(lower_nodes, upper_nodes, live_mask, counted):

    def lagrange(lower_pos, upper_pos):
        return layer_terms(lower_pos, upper_pos, lower_nodes[3:], upper_nodes[3:], live_mask, counted)
    lagrangian, pullback, volume = jax.vjp(lagrange, lower_nodes[:3], upper_nodes[:3], has_aux=True)
    grad_lower, grad_upper = pullback(jnp.ones_like(lagrangian))
    return (grad_lower, grad_upper, volume)

def reference(offsets, displacement, adjoint, span_x, span_y, span_z):
    points = control_points(offsets, NX, NY, NZ)
    basis_x = basis_matrix(span_x, 0, NX, NCX)
    basis_y = basis_matrix(span_y, 0, NY, NCY)
    basis_z = basis_matrix(span_z, 0, NZ, NCZ)
    everywhere = jnp.ones((NY - 1, NZ - 1), dtype=jnp.bool_)

    def advance(carry, layer_index):
        accumulated, volume = carry
        pair_basis = lax.dynamic_slice_in_dim(basis_x, layer_index, 2, 0)
        positions = node_positions(points, pair_basis, basis_y, basis_z)
        moved_part = lax.dynamic_slice_in_dim(displacement, layer_index, 2, 0)
        weights = lax.dynamic_slice_in_dim(adjoint, layer_index, 2, 0)
        node_data = jnp.concatenate([positions, moved_part, weights], axis=1)
        grad_lower, grad_upper, layer_volume = layer_gradient(node_data[0], node_data[1], everywhere, everywhere)
        node_grad = jnp.stack([grad_lower, grad_upper])
        accumulated = accumulated + control_terms(node_grad, pair_basis, basis_y, basis_z)
        return ((accumulated, volume + layer_volume), None)
    initial = (jnp.zeros((3, NCX, NCY, NCZ), jnp.float32), jnp.zeros((), jnp.float32))
    (accumulated, volume), unused = lax.scan(advance, initial, jnp.arange(NX - 1, dtype=jnp.int32))
    elements = (NX - 1) * (NY - 1) * (NZ - 1)
    return (accumulated * (elements / volume)).reshape(3, NCX, NCY * NCZ)
```

```python
import functools

import jax
import jax.numpy as jnp
from jax import lax
from jax.experimental import pallas as pl
from jax.experimental.pallas import tpu as pltpu
from jax.sharding import Mesh
from jax.sharding import PartitionSpec as P

NCX = 48
NCY = 64
NCZ = 64
MU_SHEAR = 40.0
LAME_RATIO = 60.0 / 40.0
TAPER_RATE = 0.8

LENGTH = ("zl", "y")
WIDTH = ("x", "c")
DEPTH = ("zh",)
F32 = jnp.float32
BF16 = jnp.bfloat16
MIB = 1 << 20


def spline_weights(t):
    c = 1.0 - t
    t2 = t * t
    t3 = t2 * t
    return [
        c * c * c / 6.0,
        (3.0 * t3 - 6.0 * t2 + 4.0) / 6.0,
        (-3.0 * t3 + 3.0 * t2 + 3.0 * t + 1.0) / 6.0,
        t3 / 6.0,
    ]


def node_params(span_ref, first, count):
    total = span_ref.shape[1]
    table = jnp.broadcast_to(span_ref[...].astype(F32), (count, total))
    place = lax.broadcasted_iota(jnp.int32, (count, total), 1)
    node = jnp.minimum(first + lax.broadcasted_iota(jnp.int32, (count, total), 0), total - 1)
    own = jnp.sum(jnp.where(place == node, table, 0.0), axis=1, keepdims=True)
    matches = table == own
    counted = jnp.sum(jnp.where(matches, 1.0, 0.0), axis=1, keepdims=True)
    earlier = jnp.sum(jnp.where(matches & (place < node), 1.0, 0.0), axis=1, keepdims=True)
    return own, (earlier + 0.5) / counted


def node_rows(own, t, columns):
    offset = columns - own
    out = jnp.zeros(columns.shape, F32)
    for k, weight in enumerate(spline_weights(t)):
        out = out + jnp.where(offset == float(k), weight, 0.0)
    return out


def element_rows(lower, upper, columns, live):
    low, high = node_rows(*lower, columns), node_rows(*upper, columns)
    return jnp.concatenate(
        [jnp.where(live, low + high, 0.0), jnp.where(live, high - low, 0.0)], axis=0
    )


def split(value):
    high = value.astype(BF16)
    return high, (value - high.astype(F32)).astype(BF16)


def dot(a, b):
    return lax.dot_general(a, b, (((1,), (0,)), ((), ())), preferred_element_type=F32)


def face_kernel(u_ref, w_ref, x_ref, y_ref, z_ref):
    layers = u_ref.shape[0]
    rows, lanes = u_ref.shape[2], u_ref.shape[3]
    lane = lax.broadcasted_iota(jnp.int32, (rows, lanes), 1)
    for f in range(6):
        source = (u_ref, w_ref)[f // 3]
        c = f % 3
        x_ref[f] = source[0, c]
        packed = jnp.zeros((rows, lanes), F32)
        for i in range(layers):
            y_ref[i, pl.ds(f, 1)] = source[i, c, pl.ds(0, 1)]
            value = source[i, c]
            packed = jnp.where(lane == i, value if i == 0 else pltpu.roll(value, i, 1), packed)
        z_ref[f] = packed
    for i in range(layers):
        y_ref[i, pl.ds(6, 2)] = jnp.zeros((2, lanes), F32)


def net_kernel(
    sx_smem, o_ref, sx_ref, sy_ref, sz_ref, q_ref, coef_ref, lin_ref, yb_ref, zb_ref, zf_ref, yf_ref
):
    window = q_ref.shape[0] - 1
    ny, nz = q_ref.shape[2:]
    nx = window - 4
    nodes_x, nodes_y, nodes_z = sx_ref.shape[1], sy_ref.shape[1], sz_ref.shape[1]
    step_x = 2.0 * nodes_x / (NCX - 3)
    step_y = 2.0 * nodes_y / (NCY - 3)
    step_z = 2.0 * nodes_z / (NCZ - 3)
    start_x = lax.axis_index(LENGTH) * nx
    start_y = lax.axis_index(WIDTH) * ny
    start_z = lax.axis_index(DEPTH) * nz
    lanes = 2 * NCZ

    rows = coef_ref.shape[1]
    own, t = node_params(sx_ref, start_x, rows)
    own_up, t_up = node_params(sx_ref, start_x + 1, rows)
    climbs = own_up > own
    low = spline_weights(t) + [jnp.zeros_like(t)]
    high = spline_weights(t_up)
    high = [
        jnp.where(climbs, high[k - 1] if k else 0.0, high[k] if k < 4 else 0.0) for k in range(5)
    ]
    dx = (own_up - own) + (t_up - t)
    rate = TAPER_RATE / (NCX - 1)
    both = (own_up + own) + (t_up + t) + 2.0
    columns = [low[k] + high[k] for k in range(5)] + [high[k] - low[k] for k in range(5)]
    columns += [4.0 * step_x * dx, 2.0 * rate * dx, 4.0 + 2.0 * rate * both]
    for k, column in enumerate(columns):
        coef_ref[k] = jnp.broadcast_to(column, (rows, lanes))

    lower = node_params(sy_ref, start_y, ny)
    upper = node_params(sy_ref, start_y + 1, ny)
    live_y = start_y + lax.broadcasted_iota(jnp.int32, (ny, lanes), 0) < nodes_y - 1
    lane = lax.broadcasted_iota(jnp.int32, (ny, lanes), 1)
    half = NCY // 2
    y_rows = element_rows(lower, upper, (lane % NCY).astype(F32), live_y)
    for r, step in enumerate((step_x, step_y, step_z)):
        hi, lo = split(step * y_rows)
        yf_ref[r] = jnp.concatenate([hi, lo[:, :NCY]], axis=1)
    paired = 2 * (lane % half) + (lane % NCY) // half
    y_rows = element_rows(lower, upper, paired.astype(F32), live_y)
    turned = jnp.transpose(jnp.concatenate([y_rows, y_rows], axis=0))[:NCY]
    hi, lo = split(turned)
    yb_ref[...] = jnp.concatenate([hi, lo[:, : 2 * ny]], axis=1)
    place = (upper[0] + lower[0]) + (upper[1] + lower[1]) + (2.0 - (NCY - 1))
    rise = (upper[0] - lower[0]) + (upper[1] - lower[1])
    live_z = start_z + lane < nodes_z - 1
    live = live_y & live_z
    lin_ref[0] = jnp.where(live, step_y * place, 0.0)
    lin_ref[1] = jnp.where(live, step_y * rise, 0.0)
    lin_ref[4] = jnp.where(live, 0.0, 1.0)
    lin_ref[5] = jnp.where(live, 1.0, 0.0)

    lower = node_params(sz_ref, start_z, nz)
    upper = node_params(sz_ref, start_z + 1, nz)
    live_z = start_z + lax.broadcasted_iota(jnp.int32, (nz, lanes), 0) < nodes_z - 1
    lane = lax.broadcasted_iota(jnp.int32, (nz, lanes), 1)
    z_rows = element_rows(lower, upper, (lane % NCZ).astype(F32), live_z)
    wide = lax.broadcasted_iota(jnp.int32, z_rows.shape, 1)
    hi, lo = split(
        jnp.concatenate(
            [jnp.where(wide < NCZ, z_rows, 0.0), jnp.where(wide < NCZ, 0.0, z_rows)], axis=0
        )
    )
    zb_ref[0] = hi
    zb_ref[1] = lo
    hi, lo = split(jnp.transpose(z_rows)[:NCZ])
    zf_ref[0] = hi
    zf_ref[1] = lo
    place = (upper[0] + lower[0]) + (upper[1] + lower[1]) + (2.0 - (NCZ - 1))
    rise = (upper[0] - lower[0]) + (upper[1] - lower[1])
    place = jnp.transpose(jnp.broadcast_to(step_z * place, (nz, lanes)))[:ny]
    rise = jnp.transpose(jnp.broadcast_to(step_z * rise, (nz, lanes)))[:ny]
    lin_ref[2] = jnp.where(live, place, 0.0)
    lin_ref[3] = jnp.where(live, rise, 0.0)

    start = jnp.minimum(sx_smem[start_x], NCX - window)

    def step(t, carry):
        for r in range(3):
            o = o_ref[r, start + t]
            along_z = dot(o, zf_ref[0]) + dot(o, zf_ref[1])
            high, low = split(along_z)
            full = dot(yf_ref[r], jnp.concatenate([high, low, high], axis=0))
            q_ref[t, 3 * r] = full[:ny, :nz]
            q_ref[t, 3 * r + 1] = full[ny:, :nz]
            q_ref[t, 3 * r + 2] = full[:ny, nz:]
        return carry

    lax.fori_loop(0, window, step, 0)
    q_ref[window] = jnp.zeros(q_ref.shape[1:], F32)


def cofactors(m):
    out = [[None] * 3 for _ in range(3)]
    for r in range(3):
        r1, r2 = (r + 1) % 3, (r + 2) % 3
        for c in range(3):
            c1, c2 = (c + 1) % 3, (c + 2) % 3
            out[r][c] = m[r1][c1] * m[r2][c2] - m[r1][c2] * m[r2][c1]
    return out


def dot3(a, b):
    return a[0] * b[0] + a[1] * b[1] + a[2] * b[2]


def column(m, c):
    return [m[0][c], m[1][c], m[2][c]]


def element_gradient(jac, grad_u, grad_w, dead):
    cof = cofactors(jac)
    det = dot3(jac[0], cof[0])
    scale = 1.0 / (det + dead)
    inv_t = [[cof[r][c] * scale for c in range(3)] for r in range(3)]
    strain = [[dot3(grad_u[r], inv_t[c]) for c in range(3)] for r in range(3)]
    virt = [[dot3(grad_w[r], inv_t[c]) for c in range(3)] for r in range(3)]
    deform = [[strain[r][c] + 1.0 if r == c else strain[r][c] for c in range(3)] for r in range(3)]
    reduced = [[deform[r][c] - virt[r][c] for c in range(3)] for r in range(3)]
    cof_d = cofactors(deform)
    det_d = dot3(deform[0], cof_d[0])
    log_d = jnp.log(det_d)
    scale_d = 1.0 / det_d
    flip = [[cof_d[r][c] * scale_d for c in range(3)] for r in range(3)]
    mixed = [[dot3(column(virt, a), column(flip, b)) for b in range(3)] for a in range(3)]
    trace = mixed[0][0] + mixed[1][1] + mixed[2][2]
    factor = 1.0 - LAME_RATIO * log_d
    shift = factor + LAME_RATIO * trace
    inner = [
        [factor * mixed[a][b] + shift if a == b else factor * mixed[a][b] for b in range(3)]
        for a in range(3)
    ]
    quad = [[None] * 3 for _ in range(3)]
    for a in range(3):
        for b in range(a, 3):
            quad[a][b] = dot3(column(reduced, a), column(reduced, b)) - dot3(
                column(virt, a), column(virt, b)
            )
            quad[b][a] = quad[a][b]
    level = (
        0.5 * (quad[0][0] + quad[1][1] + quad[2][2])
        + (0.5 * LAME_RATIO * log_d - 1.0) * log_d
        - 1.5
        + factor * (1.0 + trace)
        + LAME_RATIO * trace
    )
    tensor = [
        [reduced[a][b] - quad[a][b] - dot3(flip[a], column(inner, b)) for b in range(3)]
        for a in range(3)
    ]
    for a in range(3):
        tensor[a][a] = tensor[a][a] + level
    return det, [[dot3(tensor[r], column(cof, s)) for s in range(3)] for r in range(3)]


def element_kernel(
    sx_smem, coef_ref, u_ref, w_ref, xf_ref, yf_ref, yxf_ref, zf_ref, zxf_ref, zyf_ref, zxyf_ref,
    lin_ref, q_ref, yb_ref, zb_ref, out_ref, raw, side, sums, diffs, planes, acc, left_hi, left_lo,
):
    layers, _, ny, nz = u_ref.shape
    window = q_ref.shape[0] - 1
    start_x = lax.axis_index(LENGTH) * layers
    live_layers = jnp.minimum(layers, sx_smem.shape[0] - 1 - start_x)
    start = jnp.minimum(sx_smem[start_x], NCX - window)
    rows = ny + 8
    lane = lax.broadcasted_iota(jnp.int32, (rows, nz), 1)

    for f in range(6):
        far = pltpu.roll(zxf_ref[f], layers, 1)
        side[f, pl.ds(0, ny)] = jnp.where(lane[:ny] == layers, far, zf_ref[f])
        far = pltpu.roll(zxyf_ref[f], layers, 1)
        side[f, pl.ds(ny, 8)] = jnp.where(lane[:8] == layers, far, zyf_ref[f])
    acc[...] = jnp.zeros(acc.shape, F32)

    def make_planes(i):
        slot = lax.rem(i, 2)

        @pl.when(i < layers)
        def _():
            edge = yf_ref[i]
            for f in range(6):
                raw[f, pl.ds(0, ny)] = (u_ref, w_ref)[f // 3][i, f % 3]
                raw[f, pl.ds(ny, 1)] = edge[f : f + 1]

        @pl.when(i >= layers)
        def _():
            for f in range(6):
                raw[f, pl.ds(0, ny)] = xf_ref[f]
                raw[f, pl.ds(ny, 1)] = yxf_ref[pl.ds(f, 1)]

        for f in range(6):
            here = raw[f]
            beyond = pltpu.roll(side[f], nz - 1 - i, 1)
            there = jnp.where(lane == nz - 1, beyond, pltpu.roll(here, nz - 1, 1))
            sums[f] = here + there
            diffs[f] = there - here
        for f in range(6):
            low, high = sums[f, pl.ds(0, ny)], sums[f, pl.ds(1, ny)]
            planes[slot, 3 * f] = low + high
            planes[slot, 3 * f + 1] = high - low
            planes[slot, 3 * f + 2] = diffs[f, pl.ds(0, ny)] + diffs[f, pl.ds(1, ny)]

    raw[:, pl.ds(ny, 8)] = jnp.zeros((6, 8, nz), F32)
    make_planes(jnp.int32(0))

    def layer(i, volume):
        make_planes(i + 1)
        new, old = lax.rem(i + 1, 2), lax.rem(i, 2)
        first = sx_smem[start_x + i] - start
        coef = [coef_ref[k, pl.ds(i, 1)] for k in range(13)]
        total, delta = coef[:5], coef[5:10]
        for block in range(ny // 8):
            at = pl.ds(8 * block, 8)
            jac = [[None] * 3 for _ in range(3)]
            for r in range(3):
                for s in range(3):
                    weight = delta if s == 0 else total
                    value = weight[0] * q_ref[first, 3 * r + s, at]
                    for k in range(1, 5):
                        value = value + weight[k] * q_ref[first + k, 3 * r + s, at]
                    jac[r][s] = value
            jac[0][0] = jac[0][0] + coef[10] * lin_ref[5, at]
            jac[1][0] = jac[1][0] + coef[11] * lin_ref[0, at]
            jac[1][1] = jac[1][1] + coef[12] * lin_ref[1, at]
            jac[2][0] = jac[2][0] + coef[11] * lin_ref[2, at]
            jac[2][2] = jac[2][2] + coef[12] * lin_ref[3, at]
            grads = []
            for f in range(6):
                grads.append(
                    [
                        planes[new, 3 * f, at] - planes[old, 3 * f, at],
                        planes[new, 3 * f + 1, at] + planes[old, 3 * f + 1, at],
                        planes[new, 3 * f + 2, at] + planes[old, 3 * f + 2, at],
                    ]
                )
            det, gradient = element_gradient(jac, grads[:3], grads[3:], lin_ref[4, at])
            volume = volume + det
            for r in range(3):
                for s in range(3):
                    weight = delta if s == 0 else total
                    for k in range(5):
                        p = (first + k, 3 * r + s, at)
                        acc[p] = acc[p] + weight[k] * gradient[r][s]
        return volume

    volume = lax.fori_loop(0, live_layers, layer, jnp.zeros((8, nz), F32))

    blank = jnp.zeros((ny, nz), BF16)
    half = NCY // 2

    def along_width(t, carry):
        for r in range(3):
            hi, lo = [], []
            for s in range(3):
                h, l = split(acc[t, 3 * r + s])
                hi.append(h)
                lo.append(l)
            hi = jnp.concatenate(
                [jnp.concatenate([hi[0], hi[2]], axis=1), jnp.concatenate([hi[1], blank], axis=1)],
                axis=0,
            )
            lo = jnp.concatenate(
                [jnp.concatenate([lo[0], lo[2]], axis=1), jnp.concatenate([lo[1], blank], axis=1)],
                axis=0,
            )
            full = dot(yb_ref[...], jnp.concatenate([hi, lo, hi], axis=0))
            high, low = split(full)
            at = pl.ds(pl.multiple_of((t * 3 + r) * half, half), half)
            left_hi[at, pl.ds(0, 2 * nz)] = high[:half]
            left_hi[at, pl.ds(2 * nz, 2 * nz)] = high[half:]
            left_lo[at, pl.ds(0, 2 * nz)] = low[:half]
            left_lo[at, pl.ds(2 * nz, 2 * nz)] = low[half:]
        return carry

    lax.fori_loop(0, window, along_width, 0)

    stride = out_ref.shape[0] // half
    batch = 12

    def along_depth(step, carry):
        at = pl.ds(pl.multiple_of(step * batch * half, half), batch * half)
        hi, lo = left_hi[at], left_lo[at]
        full = dot(hi, zb_ref[0]) + dot(lo, zb_ref[0]) + dot(hi, zb_ref[1])
        for b in range(batch):
            out_ref[pl.ds(step * batch + b, half, stride=stride)] = full[b * half : (b + 1) * half]
        return carry

    lax.fori_loop(0, 3 * window // batch, along_depth, 0)

    total = jnp.sum(volume, axis=0, keepdims=True)
    out_ref[pl.ds(3 * window, half, stride=stride)] = jnp.broadcast_to(total, (half, nz))
    for spare in range(3 * window + 1, stride):
        out_ref[pl.ds(spare, half, stride=stride)] = jnp.zeros((half, nz), F32)


def shifted(value, axes, sizes):
    names = sum(axes, ())
    dims = [sizes[a] for a in axes]
    pairs = []
    count = 1
    for d in dims:
        count *= d
    for flat in range(count):
        rest, index = flat, []
        for d in reversed(dims):
            index.insert(0, rest % d)
            rest //= d
        if all(v > 0 for v in index):
            target = 0
            for v, d in zip(index, dims):
                target = target * d + v - 1
            pairs.append((flat, target))
    return lax.ppermute(value, names, pairs)


def on_device(sizes, offsets, displacement, adjoint, span_x, span_y, span_z):
    nx, _, ny, nz = displacement.shape
    nodes_x, nodes_y, nodes_z = span_x.shape[0], span_y.shape[0], span_z.shape[0]
    vmem = pl.BlockSpec(memory_space=pltpu.VMEM)
    smem = pl.BlockSpec(memory_space=pltpu.SMEM)

    x_face, y_face, z_face = pl.pallas_call(
        face_kernel,
        out_shape=(
            jax.ShapeDtypeStruct((6, ny, nz), F32),
            jax.ShapeDtypeStruct((nx, 8, nz), F32),
            jax.ShapeDtypeStruct((6, ny, nz), F32),
        ),
        in_specs=[vmem] * 2,
        out_specs=(vmem,) * 3,
        name="faces",
        compiler_params=pltpu.CompilerParams(vmem_limit_bytes=16 * MIB),
    )(displacement, adjoint)
    xf = shifted(x_face, (LENGTH,), sizes)
    yf = shifted(y_face, (WIDTH,), sizes)
    zf = shifted(z_face, (DEPTH,), sizes)
    yxf = shifted(y_face[0], (LENGTH, WIDTH), sizes)
    zxf = shifted(z_face, (LENGTH, DEPTH), sizes)
    zyf = shifted(z_face[:, :8], (WIDTH, DEPTH), sizes)
    zxyf = shifted(z_face[:, :8], (LENGTH, WIDTH, DEPTH), sizes)

    window = nx + 4
    spans = [s.reshape(1, s.shape[0]) for s in (span_x, span_y, span_z)]
    net, coef, linear, y_back, z_back = pl.pallas_call(
        net_kernel,
        out_shape=(
            jax.ShapeDtypeStruct((window + 1, 9, ny, nz), F32),
            jax.ShapeDtypeStruct((13, -(-nx // 8) * 8, nz), F32),
            jax.ShapeDtypeStruct((6, ny, nz), F32),
            jax.ShapeDtypeStruct((NCY, 6 * ny), BF16),
            jax.ShapeDtypeStruct((2, 4 * nz, 2 * NCZ), BF16),
        ),
        in_specs=[smem] + [vmem] * 4,
        out_specs=(vmem,) * 5,
        scratch_shapes=[
            pltpu.VMEM((2, NCZ, 2 * nz), BF16),
            pltpu.VMEM((3, 2 * ny, 3 * NCY), BF16),
        ],
        name="net",
        compiler_params=pltpu.CompilerParams(vmem_limit_bytes=24 * MIB),
        cost_estimate=pl.CostEstimate(flops=2 * 10**9, bytes_accessed=6 * MIB, transcendentals=0),
    )(span_x, offsets.reshape(3, NCX, NCY, NCZ), *spans)

    half = NCY // 2
    stride = -(-(3 * window + 1) // 8) * 8
    terms = pl.pallas_call(
        element_kernel,
        out_shape=jax.ShapeDtypeStruct((half * stride, 2 * NCZ), F32),
        in_specs=[smem] + [vmem] * 14,
        out_specs=vmem,
        scratch_shapes=[
            pltpu.VMEM((6, ny + 8, nz), F32),
            pltpu.VMEM((6, ny + 8, nz), F32),
            pltpu.VMEM((6, ny + 8, nz), F32),
            pltpu.VMEM((6, ny + 8, nz), F32),
            pltpu.VMEM((2, 18, ny, nz), F32),
            pltpu.VMEM((window + 1, 9, ny, nz), F32),
            pltpu.VMEM((3 * window * half, 4 * nz), BF16),
            pltpu.VMEM((3 * window * half, 4 * nz), BF16),
        ],
        name="elements",
        compiler_params=pltpu.CompilerParams(vmem_limit_bytes=48 * MIB),
        cost_estimate=pl.CostEstimate(flops=10**10, bytes_accessed=10 * MIB, transcendentals=0),
    )(
        span_x, coef, displacement, adjoint, xf, yf, yxf, zf, zxf, zyf, zxyf,
        linear, net, y_back, z_back,
    )

    size_w, size_d = sizes[WIDTH], sizes[DEPTH]
    terms = terms.reshape(size_w, size_d * stride, 2 * NCZ)
    terms = jnp.sum(lax.all_to_all(terms, WIDTH, 0, 0, tiled=True), axis=0)
    terms = terms.reshape(size_d, stride, 2 * NCZ)
    terms = jnp.sum(lax.all_to_all(terms, DEPTH, 0, 0, tiled=True), axis=0)
    size_l = sizes[LENGTH]
    part = 3 * NCX // size_l
    start = lax.dynamic_slice_in_dim(span_x, lax.axis_index(LENGTH) * nx, 1)[0]
    first_row = jnp.minimum(start, NCX - window)
    spread = lax.dynamic_update_slice(
        jnp.zeros((3 * NCX, 2 * NCZ), F32), terms[: 3 * window], (3 * first_row, 0)
    )
    spread = jnp.concatenate(
        [
            spread.reshape(size_l, part, 2 * NCZ),
            jnp.broadcast_to(terms[3 * window], (size_l, 1, 2 * NCZ)),
        ],
        axis=1,
    )
    summed = jnp.sum(lax.all_to_all(spread, LENGTH, 0, 0, tiled=True), axis=0)
    elements = (nodes_x - 1) * (nodes_y - 1) * (nodes_z - 1)
    owned = summed[:part] * (elements * MU_SHEAR / jnp.sum(summed[part]))
    size_x, size_c = size_w // 2, 2
    for axes, size in ((LENGTH, size_l), (DEPTH, size_d), (("x",), size_x)):
        owned = jnp.broadcast_to(owned[None], (size,) + owned.shape)
        owned = lax.all_to_all(owned, axes, 0, 0, tiled=True)
    other = lax.ppermute(owned, "c", [(0, 1), (1, 0)])
    core = lax.axis_index("c")
    both = jnp.stack([jnp.where(core == 0, owned, other), jnp.where(core == 0, other, owned)])
    both = both.reshape(size_c, size_x, size_d, size_l, part // 3, 3, 2 * NCZ)
    return both.transpose(5, 3, 4, 1, 0, 2, 6).reshape(3, NCX, NCY * NCZ)


def solution(mesh):
    count_x, count_y, count_z = mesh.devices.shape
    fine = Mesh(
        mesh.devices.reshape(2, count_x // 2, count_y // 2, 2, count_z), ("zl", "y", "x", "c", "zh")
    )
    sizes = {LENGTH: count_x, WIDTH: count_y, DEPTH: count_z}
    brick = P(LENGTH, None, WIDTH, DEPTH)
    return jax.shard_map(
        functools.partial(on_device, sizes),
        mesh=fine,
        in_specs=(P(), brick, brick, P(), P(), P()),
        out_specs=P(),
        check_vma=False,
    )
```

```python
import functools

import jax
import jax.numpy as jnp
from jax import lax
from jax.experimental import pallas as pl
from jax.experimental.pallas import tpu as pltpu
from jax.sharding import Mesh
from jax.sharding import PartitionSpec as P

NCX = 48
NCY = 64
NCZ = 64
MU_SHEAR = 40.0
LAME_RATIO = 60.0 / 40.0
TAPER_RATE = 0.8

LENGTH = ("zl", "y")
WIDTH = ("x", "c")
DEPTH = ("zh",)
F32 = jnp.float32
BF16 = jnp.bfloat16
MIB = 1 << 20
FOLD = 1
DEPTH_SIZE = 4
PITCH = NCY + 1


def spline_weights(t):
    c = 1.0 - t
    t2 = t * t
    t3 = t2 * t
    return [
        c * c * c / 6.0,
        (3.0 * t3 - 6.0 * t2 + 4.0) / 6.0,
        (-3.0 * t3 + 3.0 * t2 + 3.0 * t + 1.0) / 6.0,
        t3 / 6.0,
    ]


def node_params(span_ref, first, count):
    total = span_ref.shape[1]
    table = jnp.broadcast_to(span_ref[...].astype(F32), (count, total))
    place = lax.broadcasted_iota(jnp.int32, (count, total), 1)
    node = jnp.minimum(first + lax.broadcasted_iota(jnp.int32, (count, total), 0), total - 1)
    own = jnp.sum(jnp.where(place == node, table, 0.0), axis=1, keepdims=True)
    matches = table == own
    counted = jnp.sum(jnp.where(matches, 1.0, 0.0), axis=1, keepdims=True)
    earlier = jnp.sum(jnp.where(matches & (place < node), 1.0, 0.0), axis=1, keepdims=True)
    return own, (earlier + 0.5) / counted


def node_rows(own, t, columns):
    offset = columns - own
    out = jnp.zeros(columns.shape, F32)
    for k, weight in enumerate(spline_weights(t)):
        out = out + jnp.where(offset == float(k), weight, 0.0)
    return out


def element_rows(lower, upper, columns, live):
    low, high = node_rows(*lower, columns), node_rows(*upper, columns)
    return jnp.concatenate(
        [jnp.where(live, low + high, 0.0), jnp.where(live, high - low, 0.0)], axis=0
    )


def split(value):
    high = value.astype(BF16)
    return high, (value - high.astype(F32)).astype(BF16)


def dot(a, b):
    return lax.dot_general(a, b, (((1,), (0,)), ((), ())), preferred_element_type=F32)


def face_kernel(u_ref, w_ref, y_ref, z_ref):
    layers = u_ref.shape[0]
    rows, lanes = u_ref.shape[2], u_ref.shape[3]
    lane = lax.broadcasted_iota(jnp.int32, (rows, lanes), 1)
    for f in range(6):
        source = (u_ref, w_ref)[f // 3]
        c = f % 3
        packed = jnp.zeros((rows, lanes), F32)
        for i in range(layers):
            y_ref[i, pl.ds(f, 1)] = source[i, c, pl.ds(0, 1)]
            value = source[i, c]
            packed = jnp.where(lane == i, value if i == 0 else pltpu.roll(value, i, 1), packed)
        z_ref[f] = packed
    for i in range(layers):
        y_ref[i, pl.ds(6, 2)] = jnp.zeros((2, lanes), F32)


def widen_kernel(y_ref, xf_ref, out_ref):
    layers = y_ref.shape[0]
    out_ref[pl.ds(0, layers)] = y_ref[...]
    for f in range(6):
        out_ref[layers, pl.ds(f, 1)] = xf_ref[f, pl.ds(0, 1)]
    out_ref[layers, pl.ds(6, 2)] = jnp.zeros((2, out_ref.shape[2]), F32)


def deepen_kernel(z_ref, xf_ref, yf_ref, out_ref):
    layers = yf_ref.shape[0] - 1
    rows, lanes = z_ref.shape[1:]
    lane = lax.broadcasted_iota(jnp.int32, (rows, lanes), 1)
    edge = jnp.zeros((8, lanes), F32)
    for i in range(layers + 1):
        value = yf_ref[i]
        edge = jnp.where(lane[:8] == i, value if i == 0 else pltpu.roll(value, i, 1), edge)
    for f in range(6):
        far = pltpu.roll(xf_ref[f], layers, 1)
        out_ref[f, pl.ds(0, rows)] = jnp.where(lane == layers, far, z_ref[f])
        out_ref[f, pl.ds(rows, 8)] = jnp.broadcast_to(edge[f : f + 1], (8, lanes))


def table_kernel(
    nx, sx_ref, sy_ref, sz_ref, coef_ref, lin_ref, yb_ref, zb_ref, zf_ref, yf_ref
):
    ny, nz = lin_ref.shape[1:]
    nodes_x, nodes_y, nodes_z = sx_ref.shape[1], sy_ref.shape[1], sz_ref.shape[1]
    step_x = 2.0 * nodes_x / (NCX - 3)
    step_y = 2.0 * nodes_y / (NCY - 3)
    step_z = 2.0 * nodes_z / (NCZ - 3)
    start_x = lax.axis_index(LENGTH) * nx
    start_y = lax.axis_index(WIDTH) * ny
    start_z = lax.axis_index(DEPTH) * nz
    lanes = 2 * NCZ

    rows = coef_ref.shape[1]
    own, t = node_params(sx_ref, start_x, rows)
    own_up, t_up = node_params(sx_ref, start_x + 1, rows)
    climbs = own_up > own
    low = spline_weights(t) + [jnp.zeros_like(t)]
    high = spline_weights(t_up)
    high = [
        jnp.where(climbs, high[k - 1] if k else 0.0, high[k] if k < 4 else 0.0) for k in range(5)
    ]
    dx = (own_up - own) + (t_up - t)
    rate = TAPER_RATE / (NCX - 1)
    both = (own_up + own) + (t_up + t) + 2.0
    columns = [low[k] + high[k] for k in range(5)] + [high[k] - low[k] for k in range(5)]
    columns += [4.0 * step_x * dx, 2.0 * rate * dx, 4.0 + 2.0 * rate * both]
    for k, column in enumerate(columns):
        coef_ref[k] = jnp.broadcast_to(column, (rows, lanes))

    lower = node_params(sy_ref, start_y, ny)
    upper = node_params(sy_ref, start_y + 1, ny)
    live_y = start_y + lax.broadcasted_iota(jnp.int32, (ny, lanes), 0) < nodes_y - 1
    lane = lax.broadcasted_iota(jnp.int32, (ny, lanes), 1)
    half = NCY // 2
    y_rows = element_rows(lower, upper, (lane % NCY).astype(F32), live_y)
    for r, step in enumerate((step_x, step_y, step_z)):
        hi, lo = split(step * y_rows)
        some = jnp.concatenate([hi, lo[:, :NCY]], axis=1)
        none = jnp.zeros_like(some)
        yf_ref[r] = jnp.concatenate(
            [
                jnp.concatenate([some if g == h else none for h in range(FOLD)], axis=1)
                for g in range(FOLD)
            ],
            axis=0,
        )
    place = lane % half
    core = (lax.axis_index("c") + 2 * place // half) % 2
    owner = (place % (half // 2)) // DEPTH_SIZE * 2 + core
    paired = 2 * (owner * DEPTH_SIZE + place % DEPTH_SIZE) + (lane % NCY) // half
    y_rows = element_rows(lower, upper, paired.astype(F32), live_y)
    turned = jnp.transpose(jnp.concatenate([y_rows, y_rows], axis=0))[:NCY]
    hi, lo = split(turned)
    yb_ref[...] = jnp.concatenate([hi, lo[:, : 2 * ny]], axis=1)
    place = (upper[0] + lower[0]) + (upper[1] + lower[1]) + (2.0 - (NCY - 1))
    rise = (upper[0] - lower[0]) + (upper[1] - lower[1])
    live_z = start_z + lane < nodes_z - 1
    live = live_y & live_z
    lin_ref[0] = jnp.where(live, step_y * place, 0.0)
    lin_ref[1] = jnp.where(live, step_y * rise, 0.0)
    lin_ref[4] = jnp.where(live, 0.0, 1.0)
    lin_ref[5] = jnp.where(live, 1.0, 0.0)

    lower = node_params(sz_ref, start_z, nz)
    upper = node_params(sz_ref, start_z + 1, nz)
    live_z = start_z + lax.broadcasted_iota(jnp.int32, (nz, lanes), 0) < nodes_z - 1
    lane = lax.broadcasted_iota(jnp.int32, (nz, lanes), 1)
    z_rows = element_rows(lower, upper, (lane % NCZ).astype(F32), live_z)
    wide = lax.broadcasted_iota(jnp.int32, z_rows.shape, 1)
    hi, lo = split(
        jnp.concatenate(
            [jnp.where(wide < NCZ, z_rows, 0.0), jnp.where(wide < NCZ, 0.0, z_rows)], axis=0
        )
    )
    zb_ref[...] = jnp.concatenate([hi, lo], axis=1)
    turned = jnp.transpose(z_rows)
    tall = lax.broadcasted_iota(jnp.int32, turned.shape, 0) < NCZ
    hi, lo = split(
        jnp.concatenate([jnp.where(tall, turned, 0.0), jnp.where(tall, 0.0, turned)], axis=1)
    )
    zf_ref[...] = jnp.concatenate([hi, lo], axis=0)
    place = (upper[0] + lower[0]) + (upper[1] + lower[1]) + (2.0 - (NCZ - 1))
    rise = (upper[0] - lower[0]) + (upper[1] - lower[1])
    place = jnp.transpose(jnp.broadcast_to(step_z * place, (nz, lanes)))[:ny]
    rise = jnp.transpose(jnp.broadcast_to(step_z * rise, (nz, lanes)))[:ny]
    lin_ref[2] = jnp.where(live, place, 0.0)
    lin_ref[3] = jnp.where(live, rise, 0.0)


def net_kernel(sx_smem, o_ref, zf_ref, yf_ref, q_ref, plain_ref, slope_ref):
    window = q_ref.shape[0] - 1
    ny, nz = q_ref.shape[2:]
    lanes = 2 * NCZ
    half = NCY // 2
    start_x = lax.axis_index(LENGTH) * (window - 4)
    group = 8

    def along_z(step, carry):
        r = step // (half // group)
        pair = lax.rem(step, half // group) * group
        wide = [
            o_ref[r, :, pl.ds(pl.multiple_of((pair + g) * lanes, lanes), lanes)]
            for g in range(group)
        ]
        wide = jnp.concatenate(wide, axis=0)
        full = dot(jnp.concatenate([wide, wide], axis=1), zf_ref[...])
        for g in range(group):
            part = full[g * NCX : (g + 1) * NCX]
            for p in range(2):
                rows = pl.ds(r * NCX * PITCH + 2 * (pair + g) + p, NCX, stride=PITCH)
                plain_ref[rows] = part[:, 2 * p * nz : (2 * p + 1) * nz]
                slope_ref[rows] = part[:, (2 * p + 1) * nz : (2 * p + 2) * nz]
        return carry

    lax.fori_loop(0, 3 * half // group, along_z, 0)

    start = jnp.minimum(sx_smem[start_x], NCX - window)

    def along_y(step, carry):
        for r in range(3):
            both = []
            for g in range(FOLD):
                rows = pl.ds((r * NCX + start + step * FOLD + g) * PITCH, NCY)
                hi, lo = split(jnp.concatenate([plain_ref[rows], slope_ref[rows]], axis=1))
                both += [hi, lo, hi]
            full = dot(yf_ref[r], jnp.concatenate(both, axis=0))
            for g in range(FOLD):
                part = full[g * 2 * ny : (g + 1) * 2 * ny]
                q_ref[step * FOLD + g, 3 * r] = part[:ny, :nz]
                q_ref[step * FOLD + g, 3 * r + 1] = part[ny:, :nz]
                q_ref[step * FOLD + g, 3 * r + 2] = part[:ny, nz:]
        return carry

    lax.fori_loop(0, window // FOLD, along_y, 0, unroll=4)
    q_ref[window] = jnp.zeros(q_ref.shape[1:], F32)


def cofactors(m):
    out = [[None] * 3 for _ in range(3)]
    for r in range(3):
        r1, r2 = (r + 1) % 3, (r + 2) % 3
        for c in range(3):
            c1, c2 = (c + 1) % 3, (c + 2) % 3
            out[r][c] = m[r1][c1] * m[r2][c2] - m[r1][c2] * m[r2][c1]
    return out


def dot3(a, b):
    return a[0] * b[0] + a[1] * b[1] + a[2] * b[2]


def column(m, c):
    return [m[0][c], m[1][c], m[2][c]]


def element_gradient(jac, grad_u, grad_w, dead):
    cof = cofactors(jac)
    det = dot3(jac[0], cof[0])
    scale = 1.0 / (det + dead)
    inv_t = [[cof[r][c] * scale for c in range(3)] for r in range(3)]
    strain = [[dot3(grad_u[r], inv_t[c]) for c in range(3)] for r in range(3)]
    virt = [[dot3(grad_w[r], inv_t[c]) for c in range(3)] for r in range(3)]
    deform = [[strain[r][c] + 1.0 if r == c else strain[r][c] for c in range(3)] for r in range(3)]
    reduced = [[deform[r][c] - virt[r][c] for c in range(3)] for r in range(3)]
    cof_d = cofactors(deform)
    det_d = dot3(deform[0], cof_d[0])
    log_d = jnp.log(det_d)
    scale_d = 1.0 / det_d
    flip = [[cof_d[r][c] * scale_d for c in range(3)] for r in range(3)]
    mixed = [[dot3(column(virt, a), column(flip, b)) for b in range(3)] for a in range(3)]
    trace = mixed[0][0] + mixed[1][1] + mixed[2][2]
    factor = 1.0 - LAME_RATIO * log_d
    shift = factor + LAME_RATIO * trace
    inner = [
        [factor * mixed[a][b] + shift if a == b else factor * mixed[a][b] for b in range(3)]
        for a in range(3)
    ]
    quad = [[None] * 3 for _ in range(3)]
    for a in range(3):
        for b in range(a, 3):
            quad[a][b] = dot3(column(reduced, a), column(reduced, b)) - dot3(
                column(virt, a), column(virt, b)
            )
            quad[b][a] = quad[a][b]
    level = (
        0.5 * (quad[0][0] + quad[1][1] + quad[2][2])
        + (0.5 * LAME_RATIO * log_d - 1.0) * log_d
        - 1.5
        + factor * (1.0 + trace)
        + LAME_RATIO * trace
    )
    tensor = [
        [reduced[a][b] - quad[a][b] - dot3(flip[a], column(inner, b)) for b in range(3)]
        for a in range(3)
    ]
    for a in range(3):
        tensor[a][a] = tensor[a][a] + level
    return det, [[dot3(tensor[r], column(cof, s)) for s in range(3)] for r in range(3)]


def element_kernel(
    sx_smem, coef_ref, u_ref, w_ref, xf_ref, yf_ref, zf_ref, lin_ref, q_ref, yb_ref, zb_ref,
    keep_ref, send_ref, raw, sums, diffs, planes, acc, left_hi, left_lo, stage,
):
    layers, _, ny, nz = u_ref.shape
    window = q_ref.shape[0] - 1
    start_x = lax.axis_index(LENGTH) * layers
    live_layers = jnp.minimum(layers, sx_smem.shape[0] - 1 - start_x)
    start = jnp.minimum(sx_smem[start_x], NCX - window)
    rows = ny + 8
    lane = lax.broadcasted_iota(jnp.int32, (rows, nz), 1)

    acc[...] = jnp.zeros(acc.shape, F32)

    def make_planes(i):
        slot = lax.rem(i, 2)

        edge = yf_ref[i]
        for f in range(6):
            raw[f, pl.ds(ny, 1)] = edge[f : f + 1]

        @pl.when(i < layers)
        def _():
            for f in range(6):
                raw[f, pl.ds(0, ny)] = (u_ref, w_ref)[f // 3][i, f % 3]

        @pl.when(i >= layers)
        def _():
            for f in range(6):
                raw[f, pl.ds(0, ny)] = xf_ref[f]

        for f in range(6):
            here = raw[f]
            beyond = pltpu.roll(zf_ref[f], nz - 1 - i, 1)
            there = jnp.where(lane == nz - 1, beyond, pltpu.roll(here, nz - 1, 1))
            sums[f] = here + there
            diffs[f] = there - here
        for f in range(6):
            low, high = sums[f, pl.ds(0, ny)], sums[f, pl.ds(1, ny)]
            planes[slot, 3 * f] = low + high
            planes[slot, 3 * f + 1] = high - low
            planes[slot, 3 * f + 2] = diffs[f, pl.ds(0, ny)] + diffs[f, pl.ds(1, ny)]

    raw[:, pl.ds(ny, 8)] = jnp.zeros((6, 8, nz), F32)
    make_planes(jnp.int32(0))

    def layer(i, volume):
        make_planes(i + 1)
        new, old = lax.rem(i + 1, 2), lax.rem(i, 2)
        first = sx_smem[start_x + i] - start
        coef = [coef_ref[k, pl.ds(i, 1)] for k in range(13)]
        total, delta = coef[:5], coef[5:10]
        for block in range(ny // 8):
            at = pl.ds(8 * block, 8)
            jac = [[None] * 3 for _ in range(3)]
            for r in range(3):
                for s in range(3):
                    weight = delta if s == 0 else total
                    value = weight[0] * q_ref[first, 3 * r + s, at]
                    for k in range(1, 5):
                        value = value + weight[k] * q_ref[first + k, 3 * r + s, at]
                    jac[r][s] = value
            jac[0][0] = jac[0][0] + coef[10] * lin_ref[5, at]
            jac[1][0] = jac[1][0] + coef[11] * lin_ref[0, at]
            jac[1][1] = jac[1][1] + coef[12] * lin_ref[1, at]
            jac[2][0] = jac[2][0] + coef[11] * lin_ref[2, at]
            jac[2][2] = jac[2][2] + coef[12] * lin_ref[3, at]
            grads = []
            for f in range(6):
                grads.append(
                    [
                        planes[new, 3 * f, at] - planes[old, 3 * f, at],
                        planes[new, 3 * f + 1, at] + planes[old, 3 * f + 1, at],
                        planes[new, 3 * f + 2, at] + planes[old, 3 * f + 2, at],
                    ]
                )
            det, gradient = element_gradient(jac, grads[:3], grads[3:], lin_ref[4, at])
            volume = volume + det
            for r in range(3):
                for s in range(3):
                    weight = delta if s == 0 else total
                    for k in range(5):
                        p = (first + k, 3 * r + s, at)
                        acc[p] = acc[p] + weight[k] * gradient[r][s]
        return volume

    volume = lax.fori_loop(0, live_layers, layer, jnp.zeros((8, nz), F32))

    blank = jnp.zeros((ny, nz), BF16)
    half = NCY // 2

    def along_width(t, carry):
        for r in range(3):
            hi, lo = [], []
            for s in range(3):
                h, l = split(acc[t, 3 * r + s])
                hi.append(h)
                lo.append(l)
            hi = jnp.concatenate(
                [jnp.concatenate([hi[0], hi[2]], axis=1), jnp.concatenate([hi[1], blank], axis=1)],
                axis=0,
            )
            lo = jnp.concatenate(
                [jnp.concatenate([lo[0], lo[2]], axis=1), jnp.concatenate([lo[1], blank], axis=1)],
                axis=0,
            )
            full = dot(yb_ref[...], jnp.concatenate([hi, lo, hi], axis=0))
            high, low = split(full)
            at = pl.ds(pl.multiple_of((t * 3 + r) * half, half), half)
            left_hi[at, pl.ds(0, 2 * nz)] = high[:half]
            left_hi[at, pl.ds(2 * nz, 2 * nz)] = high[half:]
            left_lo[at, pl.ds(0, 2 * nz)] = low[:half]
            left_lo[at, pl.ds(2 * nz, 2 * nz)] = low[half:]
        return carry

    lax.fori_loop(0, window, along_width, 0)

    kept = half // 2
    rows_out = keep_ref.shape[0] // kept
    pitch = rows_out + 1
    batch = 12

    def along_depth(step, carry):
        at = pl.ds(pl.multiple_of(step * batch * half, half), batch * half)
        full = dot(left_hi[at], zb_ref[...])
        full = full[:, : 2 * NCZ] + full[:, 2 * NCZ :] + dot(left_lo[at], zb_ref[:, : 2 * NCZ])
        for b in range(batch):
            stage[pl.ds(step * batch + b, half, stride=pitch)] = full[b * half : (b + 1) * half]
        return carry

    lax.fori_loop(0, 3 * window // batch, along_depth, 0)

    total = jnp.sum(volume, axis=0, keepdims=True)
    spare = lax.broadcasted_iota(jnp.int32, (rows_out - 3 * window, nz), 0)
    last = jnp.where(spare == 0, jnp.broadcast_to(total, spare.shape), 0.0)
    for q in range(half):
        out_ref = keep_ref if q < kept else send_ref
        base = (q % kept) * rows_out
        out_ref[pl.ds(base, 3 * window)] = stage[pl.ds(q * pitch, 3 * window)]
        out_ref[pl.ds(base + 3 * window, rows_out - 3 * window)] = last


def spread_kernel(sx_smem, in_ref, out_ref, dense):
    parts, depth, rows, lanes = in_ref.shape
    blocks, each = out_ref.shape[0] // depth, out_ref.shape[1] - 8
    owners = lax.axis_size(LENGTH)
    nx = sx_smem.shape[0] // owners
    window = nx + 4
    start = jnp.minimum(sx_smem[lax.axis_index(LENGTH) * nx], NCX - window)
    dense[...] = jnp.zeros(dense.shape, F32)
    row = lax.broadcasted_iota(jnp.int32, (8, lanes), 0)
    for d in range(depth):
        total = in_ref[0, d]
        for p in range(1, parts):
            total = total + in_ref[p, d]
        dense[pl.ds(3 * start, 3 * window)] = total[: 3 * window]
        last = jnp.where(row == 0, total[3 * window : 3 * window + 1], 0.0)
        for block in range(blocks):
            at = block * depth + d
            out_ref[at, pl.ds(0, each)] = dense[pl.ds(block * each, each)]
            out_ref[at, pl.ds(each, 8)] = last


def divide_kernel(in_ref, out_ref, total):
    value = in_ref[0]
    for p in range(1, in_ref.shape[0]):
        value = value + in_ref[p]
    total[...] = value
    owners = out_ref.shape[0]
    rows = in_ref.shape[1] - 8
    each = rows // owners
    for owner in range(owners):
        out_ref[owner, pl.ds(0, each)] = total[pl.ds(owner * each, each)]
        out_ref[owner, pl.ds(each, 16 - each)] = total[pl.ds(rows, 16 - each)]


def scale_kernel(elements, part, in_ref, out_ref):
    total = in_ref[0]
    for p in range(1, in_ref.shape[0]):
        total = total + in_ref[p]
    volume = jnp.sum(total[part : part + 1], axis=1, keepdims=True)
    total = total * (elements * MU_SHEAR / volume)
    for p in range(in_ref.shape[0]):
        out_ref[p] = total


def pack_kernel(in_ref, out_ref):
    owners = in_ref.shape[0]
    each = out_ref.shape[1] // owners
    for copy in range(out_ref.shape[0]):
        for owner in range(owners):
            out_ref[copy, pl.ds(owner * each, each)] = in_ref[owner, pl.ds(0, each)]


def repack_kernel(in_ref, out_ref, plane):
    copies, blocks, rows, lanes = out_ref.shape
    depth = blocks // 3
    parts = in_ref.shape[0] // depth
    each = rows // parts
    for r in range(3):
        for d in range(depth):
            for part in range(parts):
                plane[pl.ds(part * each, each)] = in_ref[part * depth + d, pl.ds(r, each, stride=3)]
            value = plane[...]
            for copy in range(copies):
                out_ref[copy, r * depth + d] = value


def place_kernel(own_ref, other_ref, out_ref):
    chips, blocks, rows, lanes = own_ref.shape
    depth = blocks // 3
    core = lax.axis_index("c")
    for ref, c in ((own_ref, core), (other_ref, 1 - core)):
        for x in range(chips):
            for r in range(3):
                for d in range(depth):
                    at = ((2 * x + c) * depth + d) * lanes
                    out_ref[r, :, pl.ds(pl.multiple_of(at, lanes), lanes)] = ref[x, r * depth + d]


def shifted(value, axes, sizes):
    return lax.ppermute(value, axes, [(i, i - 1) for i in range(1, sizes[axes])])


VMEM = pl.BlockSpec(memory_space=pltpu.VMEM)
SMEM = pl.BlockSpec(memory_space=pltpu.SMEM)


def call(kernel, out_shape, *operands, scratch=(), limit=16, flops=10**6):
    return pl.pallas_call(
        kernel,
        out_shape=out_shape,
        in_specs=[SMEM if o.ndim == 1 else VMEM for o in operands],
        out_specs=jax.tree.map(lambda _: VMEM, out_shape),
        scratch_shapes=[pltpu.VMEM(shape, dtype) for shape, dtype in scratch],
        name=getattr(kernel, "func", kernel).__name__.removesuffix("_kernel"),
        compiler_params=pltpu.CompilerParams(vmem_limit_bytes=limit * MIB),
        cost_estimate=pl.CostEstimate(flops=flops, bytes_accessed=MIB, transcendentals=0),
    )(*operands)


def array(*shape, dtype=F32):
    return jax.ShapeDtypeStruct(shape, dtype)


def brick_faces(displacement, adjoint):
    nx, _, ny, nz = displacement.shape
    return call(face_kernel, (array(nx, 8, nz), array(6, ny, nz)), displacement, adjoint)


def brick_tables(shape, span_x, span_y, span_z):
    nx, _, ny, nz = shape
    return call(
        functools.partial(table_kernel, nx),
        (
            array(13, -(-nx // 8) * 8, nz),
            array(6, ny, nz),
            array(NCY, 6 * ny, dtype=BF16),
            array(4 * nz, 4 * NCZ, dtype=BF16),
            array(4 * NCZ, 4 * nz, dtype=BF16),
            array(3, FOLD * 2 * ny, FOLD * 3 * NCY, dtype=BF16),
        ),
        *[s.reshape(1, s.shape[0]) for s in (span_x, span_y, span_z)],
        flops=10**7,
    )


def brick_net(shape, offsets, span_x, z_front, y_front):
    nx, _, ny, nz = shape
    return call(
        net_kernel,
        array(nx + 5, 9, ny, nz),
        span_x,
        offsets,
        z_front,
        y_front,
        scratch=[((3 * NCX * PITCH, nz), F32)] * 2,
        limit=20,
        flops=2 * 10**9,
    )


def brick_terms(span_x, tables, net, displacement, adjoint, halos):
    nx, _, ny, nz = displacement.shape
    coef, linear, y_back, z_back = tables[:4]
    window = nx + 4
    half = NCY // 2
    stride = -(-(3 * window + 1) // 8) * 8
    return pl.pallas_call(
        element_kernel,
        out_shape=(jax.ShapeDtypeStruct((half // 2 * stride, 2 * NCZ), F32),) * 2,
        in_specs=[SMEM] + [VMEM] * 10,
        out_specs=(VMEM,) * 2,
        scratch_shapes=[
            pltpu.VMEM((6, ny + 8, nz), F32),
            pltpu.VMEM((6, ny + 8, nz), F32),
            pltpu.VMEM((6, ny + 8, nz), F32),
            pltpu.VMEM((2, 18, ny, nz), F32),
            pltpu.VMEM((window + 1, 9, ny, nz), F32),
            pltpu.VMEM((3 * window * half, 4 * nz), BF16),
            pltpu.VMEM((3 * window * half, 4 * nz), BF16),
            pltpu.VMEM((half * (stride + 1), 2 * NCZ), F32),
        ],
        name="elements",
        compiler_params=pltpu.CompilerParams(vmem_limit_bytes=24 * MIB),
        cost_estimate=pl.CostEstimate(flops=10**10, bytes_accessed=10 * MIB, transcendentals=0),
    )(span_x, coef, displacement, adjoint, *halos, linear, net, y_back, z_back)


def on_device(sizes, offsets, displacement, adjoint, span_x, span_y, span_z):
    nodes_x, nodes_y, nodes_z = span_x.shape[0], span_y.shape[0], span_z.shape[0]
    nx, _, ny, nz = shape = displacement.shape
    swap = [(0, 1), (1, 0)]

    xf = shifted(jnp.concatenate([displacement[0], adjoint[0]], axis=0), LENGTH, sizes)
    y_face, z_face = brick_faces(displacement, adjoint)
    tables = brick_tables(shape, span_x, span_y, span_z)
    yf = shifted(call(widen_kernel, array(nx + 1, 8, nz), y_face, xf), WIDTH, sizes)
    net = brick_net(shape, offsets, span_x, *tables[4:])
    zf = shifted(call(deepen_kernel, array(6, ny + 8, nz), z_face, xf, yf), DEPTH, sizes)
    keep, send = brick_terms(span_x, tables, net, displacement, adjoint, (xf, yf, zf))

    size_l, size_w, size_d = sizes[LENGTH], sizes[WIDTH], sizes[DEPTH]
    size_x, size_zl = size_w // 2, 2
    lanes = 2 * NCZ
    stride = keep.shape[0] // (size_x * size_d)
    size_y = size_l // size_zl
    blocks, part = size_zl * size_d, 3 * NCX // size_l
    terms = keep + lax.ppermute(send, "c", swap)
    terms = lax.all_to_all(terms.reshape(size_x, size_d * stride, lanes), "x", 0, 0, tiled=True)
    terms = call(
        spread_kernel,
        array(blocks, part * size_y + 8, lanes),
        span_x,
        terms.reshape(size_x, size_d, stride, lanes),
        scratch=[((3 * NCX, lanes), F32)],
    )
    terms = lax.all_to_all(terms, ("zl", "zh"), 0, 0, tiled=True)
    terms = call(
        divide_kernel,
        array(size_y, 16, lanes),
        terms,
        scratch=[((part * size_y + 8, lanes), F32)],
    )
    terms = lax.all_to_all(terms, "y", 0, 0, tiled=True)
    elements = (nodes_x - 1) * (nodes_y - 1) * (nodes_z - 1)
    rows = call(
        functools.partial(scale_kernel, elements, part), array(size_y, 16, lanes), terms
    )
    rows = lax.all_to_all(rows, "y", 0, 0, tiled=True)
    rows = call(pack_kernel, array(blocks, part * size_y, lanes), rows)
    rows = lax.all_to_all(rows, ("zl", "zh"), 0, 0, tiled=True)
    rows = call(
        repack_kernel,
        array(size_x, 3 * size_d, NCX, lanes),
        rows,
        scratch=[((NCX, lanes), F32)],
    )
    rows = lax.all_to_all(rows, "x", 0, 0, tiled=True)
    other = lax.ppermute(rows, "c", swap)
    return call(place_kernel, array(3, NCX, NCY * NCZ), rows, other)


def solution(mesh):
    count_x, count_y, count_z = mesh.devices.shape
    fine = Mesh(
        mesh.devices.reshape(2, count_x // 2, count_y // 2, 2, count_z), ("zl", "y", "x", "c", "zh")
    )
    sizes = {LENGTH: count_x, WIDTH: count_y, DEPTH: count_z}
    brick = P(LENGTH, None, WIDTH, DEPTH)
    return jax.shard_map(
        functools.partial(on_device, sizes),
        mesh=fine,
        in_specs=(P(), brick, brick, P(), P(), P()),
        out_specs=P(),
        check_vma=False,
    )
```

```python
import functools

import jax
import jax.numpy as jnp
from jax import lax
from jax.experimental import pallas as pl
from jax.experimental.pallas import tpu as pltpu
from jax.sharding import Mesh
from jax.sharding import PartitionSpec as P

NCX = 48
NCY = 64
NCZ = 64
MU_SHEAR = 40.0
LAME_RATIO = 60.0 / 40.0
TAPER_RATE = 0.8

LENGTH = ("zl", "y")
WIDTH = ("x", "c")
DEPTH = ("zh",)
F32 = jnp.float32
BF16 = jnp.bfloat16
MIB = 1 << 20
FOLD = 1
DEPTH_SIZE = 4
PITCH = NCY + 1


def spline_weights(t):
    c = 1.0 - t
    t2 = t * t
    t3 = t2 * t
    return [
        c * c * c / 6.0,
        (3.0 * t3 - 6.0 * t2 + 4.0) / 6.0,
        (-3.0 * t3 + 3.0 * t2 + 3.0 * t + 1.0) / 6.0,
        t3 / 6.0,
    ]


def node_params(span_ref, first, count):
    total = span_ref.shape[1]
    table = jnp.broadcast_to(span_ref[...].astype(F32), (count, total))
    place = lax.broadcasted_iota(jnp.int32, (count, total), 1)
    node = jnp.minimum(first + lax.broadcasted_iota(jnp.int32, (count, total), 0), total - 1)
    own = jnp.sum(jnp.where(place == node, table, 0.0), axis=1, keepdims=True)
    matches = table == own
    counted = jnp.sum(jnp.where(matches, 1.0, 0.0), axis=1, keepdims=True)
    earlier = jnp.sum(jnp.where(matches & (place < node), 1.0, 0.0), axis=1, keepdims=True)
    return own, (earlier + 0.5) / counted


def node_rows(own, t, columns):
    offset = columns - own
    out = jnp.zeros(columns.shape, F32)
    for k, weight in enumerate(spline_weights(t)):
        out = out + jnp.where(offset == float(k), weight, 0.0)
    return out


def element_rows(lower, upper, columns, live):
    low, high = node_rows(*lower, columns), node_rows(*upper, columns)
    return jnp.concatenate(
        [jnp.where(live, low + high, 0.0), jnp.where(live, high - low, 0.0)], axis=0
    )


def split(value):
    high = value.astype(BF16)
    return high, (value - high.astype(F32)).astype(BF16)


def dot(a, b):
    return lax.dot_general(a, b, (((1,), (0,)), ((), ())), preferred_element_type=F32)


def widen_kernel(y_ref, xf_ref, out_ref):
    layers = y_ref.shape[0]
    out_ref[pl.ds(0, layers)] = y_ref[...]
    for f in range(6):
        out_ref[layers, pl.ds(f, 1)] = xf_ref[f, pl.ds(0, 1)]
    out_ref[layers, pl.ds(6, 2)] = jnp.zeros((2, out_ref.shape[2]), F32)


def deepen_kernel(z_ref, xf_ref, yf_ref, out_ref):
    layers = yf_ref.shape[0] - 1
    rows, lanes = z_ref.shape[1:]
    lane = lax.broadcasted_iota(jnp.int32, (rows, lanes), 1)
    edge = jnp.zeros((8, lanes), F32)
    for i in range(layers + 1):
        value = yf_ref[i]
        edge = jnp.where(lane[:8] == i, value if i == 0 else pltpu.roll(value, i, 1), edge)
    for f in range(6):
        far = pltpu.roll(xf_ref[f], layers, 1)
        out_ref[f, pl.ds(0, rows)] = jnp.where(lane == layers, far, z_ref[f])
        out_ref[f, pl.ds(rows, 8)] = jnp.broadcast_to(edge[f : f + 1], (8, lanes))


def pack_faces(bricks, y_ref, z_ref):
    _, layers, _, rows, lanes = bricks.shape
    lane = lax.broadcasted_iota(jnp.int32, (rows, lanes), 1)
    for f in range(6):
        packed = jnp.zeros((rows, lanes), F32)
        for i in range(layers):
            value = bricks[f // 3, i, f % 3]
            y_ref[i, pl.ds(f, 1)] = value[:1]
            packed = jnp.where(lane == i, value if i == 0 else pltpu.roll(value, i, 1), packed)
        z_ref[f] = packed
    for i in range(layers):
        y_ref[i, pl.ds(6, 2)] = jnp.zeros((2, lanes), F32)


def table_kernel(
    u_ref, w_ref, sx_ref, sy_ref, sz_ref,
    y_ref, z_ref, coef_ref, lin_ref, yb_ref, zb_ref, zf_ref, yf_ref, bricks, sems,
):
    nx = u_ref.shape[0]
    halves = ((0, nx // 2), (nx // 2, nx - nx // 2))
    copies = [
        pltpu.make_async_copy(
            ref.at[pl.ds(at, size)], bricks.at[b, pl.ds(at, size)], sems.at[2 * b + h]
        )
        for b, ref in enumerate((u_ref, w_ref))
        for h, (at, size) in enumerate(halves)
    ]
    for copy in copies:
        copy.start()
    ny, nz = lin_ref.shape[1:]
    nodes_x, nodes_y, nodes_z = sx_ref.shape[1], sy_ref.shape[1], sz_ref.shape[1]
    step_x = 2.0 * nodes_x / (NCX - 3)
    step_y = 2.0 * nodes_y / (NCY - 3)
    step_z = 2.0 * nodes_z / (NCZ - 3)
    start_x = lax.axis_index(LENGTH) * nx
    start_y = lax.axis_index(WIDTH) * ny
    start_z = lax.axis_index(DEPTH) * nz
    lanes = 2 * NCZ

    rows = coef_ref.shape[1]
    own, t = node_params(sx_ref, start_x, rows)
    own_up, t_up = node_params(sx_ref, start_x + 1, rows)
    climbs = own_up > own
    low = spline_weights(t) + [jnp.zeros_like(t)]
    high = spline_weights(t_up)
    high = [
        jnp.where(climbs, high[k - 1] if k else 0.0, high[k] if k < 4 else 0.0) for k in range(5)
    ]
    dx = (own_up - own) + (t_up - t)
    rate = TAPER_RATE / (NCX - 1)
    both = (own_up + own) + (t_up + t) + 2.0
    columns = [low[k] + high[k] for k in range(5)] + [high[k] - low[k] for k in range(5)]
    columns += [4.0 * step_x * dx, 2.0 * rate * dx, 4.0 + 2.0 * rate * both]
    for k, column in enumerate(columns):
        coef_ref[k] = jnp.broadcast_to(column, (rows, lanes))

    lower = node_params(sy_ref, start_y, ny)
    upper = node_params(sy_ref, start_y + 1, ny)
    live_y = start_y + lax.broadcasted_iota(jnp.int32, (ny, lanes), 0) < nodes_y - 1
    lane = lax.broadcasted_iota(jnp.int32, (ny, lanes), 1)
    half = NCY // 2
    y_rows = element_rows(lower, upper, (lane % NCY).astype(F32), live_y)
    for r, step in enumerate((step_x, step_y, step_z)):
        hi, lo = split(step * y_rows)
        some = jnp.concatenate([hi, lo[:, :NCY]], axis=1)
        none = jnp.zeros_like(some)
        yf_ref[r] = jnp.concatenate(
            [
                jnp.concatenate([some if g == h else none for h in range(FOLD)], axis=1)
                for g in range(FOLD)
            ],
            axis=0,
        )
    place = lane % half
    core = (lax.axis_index("c") + 2 * place // half) % 2
    owner = (place % (half // 2)) // DEPTH_SIZE * 2 + core
    paired = 2 * (owner * DEPTH_SIZE + place % DEPTH_SIZE) + (lane % NCY) // half
    y_rows = element_rows(lower, upper, paired.astype(F32), live_y)
    turned = jnp.transpose(jnp.concatenate([y_rows, y_rows], axis=0))[:NCY]
    hi, lo = split(turned)
    yb_ref[...] = jnp.concatenate([hi, lo[:, : 2 * ny]], axis=1)
    place = (upper[0] + lower[0]) + (upper[1] + lower[1]) + (2.0 - (NCY - 1))
    rise = (upper[0] - lower[0]) + (upper[1] - lower[1])
    live_z = start_z + lane < nodes_z - 1
    live = live_y & live_z
    lin_ref[0] = jnp.where(live, step_y * place, 0.0)
    lin_ref[1] = jnp.where(live, step_y * rise, 0.0)
    lin_ref[4] = jnp.where(live, 0.0, 1.0)
    lin_ref[5] = jnp.where(live, 1.0, 0.0)

    lower = node_params(sz_ref, start_z, nz)
    upper = node_params(sz_ref, start_z + 1, nz)
    live_z = start_z + lax.broadcasted_iota(jnp.int32, (nz, lanes), 0) < nodes_z - 1
    lane = lax.broadcasted_iota(jnp.int32, (nz, lanes), 1)
    z_rows = element_rows(lower, upper, (lane % NCZ).astype(F32), live_z)
    wide = lax.broadcasted_iota(jnp.int32, z_rows.shape, 1)
    hi, lo = split(
        jnp.concatenate(
            [jnp.where(wide < NCZ, z_rows, 0.0), jnp.where(wide < NCZ, 0.0, z_rows)], axis=0
        )
    )
    zb_ref[...] = jnp.concatenate([hi, lo], axis=1)
    turned = jnp.transpose(z_rows)
    tall = lax.broadcasted_iota(jnp.int32, turned.shape, 0) < NCZ
    hi, lo = split(
        jnp.concatenate([jnp.where(tall, turned, 0.0), jnp.where(tall, 0.0, turned)], axis=1)
    )
    zf_ref[...] = jnp.concatenate([hi, lo], axis=0)
    place = (upper[0] + lower[0]) + (upper[1] + lower[1]) + (2.0 - (NCZ - 1))
    rise = (upper[0] - lower[0]) + (upper[1] - lower[1])
    place = jnp.transpose(jnp.broadcast_to(step_z * place, (nz, lanes)))[:ny]
    rise = jnp.transpose(jnp.broadcast_to(step_z * rise, (nz, lanes)))[:ny]
    lin_ref[2] = jnp.where(live, place, 0.0)
    lin_ref[3] = jnp.where(live, rise, 0.0)
    for copy in copies:
        copy.wait()
    pack_faces(bricks, y_ref, z_ref)


def net_kernel(sx_smem, o_ref, zf_ref, yf_ref, q_ref, plain_ref, slope_ref):
    window = q_ref.shape[0] - 1
    ny, nz = q_ref.shape[2:]
    lanes = 2 * NCZ
    half = NCY // 2
    start_x = lax.axis_index(LENGTH) * (window - 4)
    group = 16

    def along_z(step, carry):
        r = step // (half // group)
        pair = lax.rem(step, half // group) * group
        wide = [
            o_ref[r, :, pl.ds(pl.multiple_of((pair + g) * lanes, lanes), lanes)]
            for g in range(group)
        ]
        wide = jnp.concatenate(wide, axis=0)
        full = dot(jnp.concatenate([wide, wide], axis=1), zf_ref[...])
        for g in range(group):
            part = full[g * NCX : (g + 1) * NCX]
            for p in range(2):
                rows = pl.ds(r * NCX * PITCH + 2 * (pair + g) + p, NCX, stride=PITCH)
                plain_ref[rows] = part[:, 2 * p * nz : (2 * p + 1) * nz]
                slope_ref[rows] = part[:, (2 * p + 1) * nz : (2 * p + 2) * nz]
        return carry

    lax.fori_loop(0, 3 * half // group, along_z, 0)

    start = jnp.minimum(sx_smem[start_x], NCX - window)

    def along_y(step, carry):
        for r in range(3):
            both = []
            for g in range(FOLD):
                rows = pl.ds((r * NCX + start + step * FOLD + g) * PITCH, NCY)
                hi, lo = split(jnp.concatenate([plain_ref[rows], slope_ref[rows]], axis=1))
                both += [hi, lo, hi]
            full = dot(yf_ref[r], jnp.concatenate(both, axis=0))
            for g in range(FOLD):
                part = full[g * 2 * ny : (g + 1) * 2 * ny]
                q_ref[step * FOLD + g, 3 * r] = part[:ny, :nz]
                q_ref[step * FOLD + g, 3 * r + 1] = part[ny:, :nz]
                q_ref[step * FOLD + g, 3 * r + 2] = part[:ny, nz:]
        return carry

    lax.fori_loop(0, window // FOLD, along_y, 0, unroll=7)
    q_ref[window] = jnp.zeros(q_ref.shape[1:], F32)


def cofactors(m):
    out = [[None] * 3 for _ in range(3)]
    for r in range(3):
        r1, r2 = (r + 1) % 3, (r + 2) % 3
        for c in range(3):
            c1, c2 = (c + 1) % 3, (c + 2) % 3
            out[r][c] = m[r1][c1] * m[r2][c2] - m[r1][c2] * m[r2][c1]
    return out


def dot3(a, b):
    return a[0] * b[0] + a[1] * b[1] + a[2] * b[2]


def column(m, c):
    return [m[0][c], m[1][c], m[2][c]]


def element_gradient(jac, grad_u, grad_w, dead):
    cof = cofactors(jac)
    det = dot3(jac[0], cof[0])
    scale = 1.0 / (det + dead)
    inv_t = [[cof[r][c] * scale for c in range(3)] for r in range(3)]
    strain = [[dot3(grad_u[r], inv_t[c]) for c in range(3)] for r in range(3)]
    virt = [[dot3(grad_w[r], inv_t[c]) for c in range(3)] for r in range(3)]
    deform = [[strain[r][c] + 1.0 if r == c else strain[r][c] for c in range(3)] for r in range(3)]
    reduced = [[deform[r][c] - virt[r][c] for c in range(3)] for r in range(3)]
    cof_d = cofactors(deform)
    det_d = dot3(deform[0], cof_d[0])
    log_d = jnp.log(det_d)
    scale_d = 1.0 / det_d
    flip = [[cof_d[r][c] * scale_d for c in range(3)] for r in range(3)]
    mixed = [[dot3(column(virt, a), column(flip, b)) for b in range(3)] for a in range(3)]
    trace = mixed[0][0] + mixed[1][1] + mixed[2][2]
    factor = 1.0 - LAME_RATIO * log_d
    shift = factor + LAME_RATIO * trace
    inner = [
        [factor * mixed[a][b] + shift if a == b else factor * mixed[a][b] for b in range(3)]
        for a in range(3)
    ]
    quad = [[None] * 3 for _ in range(3)]
    for a in range(3):
        for b in range(a, 3):
            quad[a][b] = dot3(column(reduced, a), column(reduced, b)) - dot3(
                column(virt, a), column(virt, b)
            )
            quad[b][a] = quad[a][b]
    level = (
        0.5 * (quad[0][0] + quad[1][1] + quad[2][2])
        + (0.5 * LAME_RATIO * log_d - 1.0) * log_d
        - 1.5
        + factor * (1.0 + trace)
        + LAME_RATIO * trace
    )
    tensor = [
        [reduced[a][b] - quad[a][b] - dot3(flip[a], column(inner, b)) for b in range(3)]
        for a in range(3)
    ]
    for a in range(3):
        tensor[a][a] = tensor[a][a] + level
    return det, [[dot3(tensor[r], column(cof, s)) for s in range(3)] for r in range(3)]


def element_kernel(
    sx_smem, coef_ref, u_ref, w_ref, xf_ref, yf_ref, zf_ref, lin_ref, q_ref, yb_ref, zb_ref,
    keep_ref, send_ref, raw, sums, diffs, planes, acc, left_hi, left_lo, stage,
):
    layers, _, ny, nz = u_ref.shape
    window = q_ref.shape[0] - 1
    start_x = lax.axis_index(LENGTH) * layers
    live_layers = jnp.minimum(layers, sx_smem.shape[0] - 1 - start_x)
    start = jnp.minimum(sx_smem[start_x], NCX - window)
    rows = ny + 8
    lane = lax.broadcasted_iota(jnp.int32, (rows, nz), 1)

    acc[...] = jnp.zeros(acc.shape, F32)

    def make_planes(i):
        slot = lax.rem(i, 2)

        edge = yf_ref[i]
        for f in range(6):
            raw[f, pl.ds(ny, 1)] = edge[f : f + 1]

        @pl.when(i < layers)
        def _():
            for f in range(6):
                raw[f, pl.ds(0, ny)] = (u_ref, w_ref)[f // 3][i, f % 3]

        @pl.when(i >= layers)
        def _():
            for f in range(6):
                raw[f, pl.ds(0, ny)] = xf_ref[f]

        for f in range(6):
            here = raw[f]
            beyond = pltpu.roll(zf_ref[f], nz - 1 - i, 1)
            there = jnp.where(lane == nz - 1, beyond, pltpu.roll(here, nz - 1, 1))
            sums[f] = here + there
            diffs[f] = there - here
        for f in range(6):
            low, high = sums[f, pl.ds(0, ny)], sums[f, pl.ds(1, ny)]
            planes[slot, 3 * f] = low + high
            planes[slot, 3 * f + 1] = high - low
            planes[slot, 3 * f + 2] = diffs[f, pl.ds(0, ny)] + diffs[f, pl.ds(1, ny)]

    raw[:, pl.ds(ny, 8)] = jnp.zeros((6, 8, nz), F32)
    make_planes(jnp.int32(0))

    def layer(i, volume):
        make_planes(i + 1)
        new, old = lax.rem(i + 1, 2), lax.rem(i, 2)
        first = sx_smem[start_x + i] - start
        coef = [coef_ref[k, pl.ds(i, 1)] for k in range(13)]
        total, delta = coef[:5], coef[5:10]
        for block in range(ny // 16):
            at = pl.ds(16 * block, 16)
            jac = [[None] * 3 for _ in range(3)]
            for r in range(3):
                for s in range(3):
                    weight = delta if s == 0 else total
                    value = weight[0] * q_ref[first, 3 * r + s, at]
                    for k in range(1, 5):
                        value = value + weight[k] * q_ref[first + k, 3 * r + s, at]
                    jac[r][s] = value
            jac[0][0] = jac[0][0] + coef[10] * lin_ref[5, at]
            jac[1][0] = jac[1][0] + coef[11] * lin_ref[0, at]
            jac[1][1] = jac[1][1] + coef[12] * lin_ref[1, at]
            jac[2][0] = jac[2][0] + coef[11] * lin_ref[2, at]
            jac[2][2] = jac[2][2] + coef[12] * lin_ref[3, at]
            grads = []
            for f in range(6):
                grads.append(
                    [
                        planes[new, 3 * f, at] - planes[old, 3 * f, at],
                        planes[new, 3 * f + 1, at] + planes[old, 3 * f + 1, at],
                        planes[new, 3 * f + 2, at] + planes[old, 3 * f + 2, at],
                    ]
                )
            det, gradient = element_gradient(jac, grads[:3], grads[3:], lin_ref[4, at])
            volume = volume + det[:8] + det[8:]
            for r in range(3):
                for s in range(3):
                    weight = delta if s == 0 else total
                    for k in range(5):
                        p = (first + k, 3 * r + s, at)
                        acc[p] = acc[p] + weight[k] * gradient[r][s]
        return volume

    volume = lax.fori_loop(0, live_layers, layer, jnp.zeros((8, nz), F32))

    blank = jnp.zeros((ny, nz), BF16)
    half = NCY // 2

    def along_width(t, carry):
        for r in range(3):
            hi, lo = [], []
            for s in range(3):
                h, l = split(acc[t, 3 * r + s])
                hi.append(h)
                lo.append(l)
            hi = jnp.concatenate(
                [jnp.concatenate([hi[0], hi[2]], axis=1), jnp.concatenate([hi[1], blank], axis=1)],
                axis=0,
            )
            lo = jnp.concatenate(
                [jnp.concatenate([lo[0], lo[2]], axis=1), jnp.concatenate([lo[1], blank], axis=1)],
                axis=0,
            )
            full = dot(yb_ref[...], jnp.concatenate([hi, lo, hi], axis=0))
            high, low = split(full)
            at = pl.ds(pl.multiple_of((t * 3 + r) * half, half), half)
            left_hi[at, pl.ds(0, 2 * nz)] = high[:half]
            left_hi[at, pl.ds(2 * nz, 2 * nz)] = high[half:]
            left_lo[at, pl.ds(0, 2 * nz)] = low[:half]
            left_lo[at, pl.ds(2 * nz, 2 * nz)] = low[half:]
        return carry

    lax.fori_loop(0, window, along_width, 0, unroll=7)

    kept = half // 2
    rows_out = keep_ref.shape[0] // kept
    pitch = rows_out + 1
    batch = 12

    def along_depth(step, carry):
        at = pl.ds(pl.multiple_of(step * batch * half, half), batch * half)
        full = dot(left_hi[at], zb_ref[...])
        full = full[:, : 2 * NCZ] + full[:, 2 * NCZ :] + dot(left_lo[at], zb_ref[:, : 2 * NCZ])
        for b in range(batch):
            stage[pl.ds(step * batch + b, half, stride=pitch)] = full[b * half : (b + 1) * half]
        return carry

    lax.fori_loop(0, 3 * window // batch, along_depth, 0, unroll=7)

    total = jnp.sum(volume, axis=0, keepdims=True)
    spare = lax.broadcasted_iota(jnp.int32, (rows_out - 3 * window, nz), 0)
    last = jnp.where(spare == 0, jnp.broadcast_to(total, spare.shape), 0.0)
    for q in range(half):
        out_ref = keep_ref if q < kept else send_ref
        base = (q % kept) * rows_out
        out_ref[pl.ds(base, 3 * window)] = stage[pl.ds(q * pitch, 3 * window)]
        out_ref[pl.ds(base + 3 * window, rows_out - 3 * window)] = last


def spread_kernel(sx_smem, in_ref, out_ref, dense):
    parts, depth, rows, lanes = in_ref.shape
    blocks, each = out_ref.shape[0] // depth, out_ref.shape[1] - 8
    owners = lax.axis_size(LENGTH)
    nx = sx_smem.shape[0] // owners
    window = nx + 4
    start = jnp.minimum(sx_smem[lax.axis_index(LENGTH) * nx], NCX - window)
    dense[...] = jnp.zeros(dense.shape, F32)
    row = lax.broadcasted_iota(jnp.int32, (8, lanes), 0)
    for d in range(depth):
        total = in_ref[0, d]
        for p in range(1, parts):
            total = total + in_ref[p, d]
        dense[pl.ds(3 * start, 3 * window)] = total[: 3 * window]
        last = jnp.where(row == 0, total[3 * window : 3 * window + 1], 0.0)
        for block in range(blocks):
            at = block * depth + d
            out_ref[at, pl.ds(0, each)] = dense[pl.ds(block * each, each)]
            out_ref[at, pl.ds(each, 8)] = last


def collect_kernel(in_ref, out_ref):
    total = in_ref[0]
    for p in range(1, in_ref.shape[0]):
        total = total + in_ref[p]
    for p in range(out_ref.shape[0]):
        out_ref[p] = total


def scale_kernel(elements, in_ref, out_ref):
    rows = out_ref.shape[1]
    total = in_ref[0]
    for p in range(1, in_ref.shape[0]):
        total = total + in_ref[p]
    volume = jnp.sum(total[rows : rows + 1], axis=1, keepdims=True)
    total = total[:rows] * (elements * MU_SHEAR / volume)
    for p in range(out_ref.shape[0]):
        out_ref[p] = total


def repack_kernel(in_ref, out_ref, plane):
    copies, blocks, rows, lanes = out_ref.shape
    depth = blocks // 3
    parts = in_ref.shape[0] // depth
    each = rows // parts
    for r in range(3):
        for d in range(depth):
            for part in range(parts):
                plane[pl.ds(part * each, each)] = in_ref[part * depth + d, pl.ds(r, each, stride=3)]
            value = plane[...]
            for copy in range(copies):
                out_ref[copy, r * depth + d] = value


def place_kernel(own_ref, other_ref, out_ref):
    chips, blocks, rows, lanes = own_ref.shape
    depth = blocks // 3
    core = lax.axis_index("c")
    for ref, c in ((own_ref, core), (other_ref, 1 - core)):
        for x in range(chips):
            for r in range(3):
                for d in range(depth):
                    at = ((2 * x + c) * depth + d) * lanes
                    out_ref[r, :, pl.ds(pl.multiple_of(at, lanes), lanes)] = ref[x, r * depth + d]


def shifted(value, axes, sizes):
    return lax.ppermute(value, axes, [(i, i - 1) for i in range(1, sizes[axes])])


VMEM = pl.BlockSpec(memory_space=pltpu.VMEM)
SMEM = pl.BlockSpec(memory_space=pltpu.SMEM)


def call(kernel, out_shape, *operands, scratch=(), limit=16, flops=10**6):
    return pl.pallas_call(
        kernel,
        out_shape=out_shape,
        in_specs=[SMEM if o.ndim == 1 else VMEM for o in operands],
        out_specs=jax.tree.map(lambda _: VMEM, out_shape),
        scratch_shapes=[pltpu.VMEM(shape, dtype) for shape, dtype in scratch],
        name=getattr(kernel, "func", kernel).__name__.removesuffix("_kernel"),
        compiler_params=pltpu.CompilerParams(vmem_limit_bytes=limit * MIB),
        cost_estimate=pl.CostEstimate(flops=flops, bytes_accessed=MIB, transcendentals=0),
    )(*operands)


def array(*shape, dtype=F32):
    return jax.ShapeDtypeStruct(shape, dtype)


def brick_tables(displacement, adjoint, span_x, span_y, span_z):
    nx, _, ny, nz = displacement.shape
    out_shape = (
        array(nx, 8, nz),
        array(6, ny, nz),
        array(13, -(-nx // 8) * 8, nz),
        array(6, ny, nz),
        array(NCY, 6 * ny, dtype=BF16),
        array(4 * nz, 4 * NCZ, dtype=BF16),
        array(4 * NCZ, 4 * nz, dtype=BF16),
        array(3, FOLD * 2 * ny, FOLD * 3 * NCY, dtype=BF16),
    )
    return pl.pallas_call(
        table_kernel,
        out_shape=out_shape,
        in_specs=[pl.BlockSpec(memory_space=pl.ANY)] * 2 + [VMEM] * 3,
        out_specs=(VMEM,) * len(out_shape),
        scratch_shapes=[
            pltpu.VMEM((2,) + displacement.shape, F32),
            pltpu.SemaphoreType.DMA((4,)),
        ],
        name="table",
        compiler_params=pltpu.CompilerParams(vmem_limit_bytes=16 * MIB),
        cost_estimate=pl.CostEstimate(flops=10**7, bytes_accessed=4 * MIB, transcendentals=0),
    )(displacement, adjoint, *[s.reshape(1, s.shape[0]) for s in (span_x, span_y, span_z)])


def brick_net(shape, offsets, span_x, z_front, y_front):
    nx, _, ny, nz = shape
    return call(
        net_kernel,
        array(nx + 5, 9, ny, nz),
        span_x,
        offsets,
        z_front,
        y_front,
        scratch=[((3 * NCX * PITCH, nz), F32)] * 2,
        limit=20,
        flops=2 * 10**9,
    )


def brick_terms(span_x, tables, net, displacement, adjoint, halos):
    nx, _, ny, nz = displacement.shape
    coef, linear, y_back, z_back = tables[:4]
    window = nx + 4
    half = NCY // 2
    stride = -(-(3 * window + 1) // 8) * 8
    return pl.pallas_call(
        element_kernel,
        out_shape=(jax.ShapeDtypeStruct((half // 2 * stride, 2 * NCZ), F32),) * 2,
        in_specs=[SMEM] + [VMEM] * 10,
        out_specs=(VMEM,) * 2,
        scratch_shapes=[
            pltpu.VMEM((6, ny + 8, nz), F32),
            pltpu.VMEM((6, ny + 8, nz), F32),
            pltpu.VMEM((6, ny + 8, nz), F32),
            pltpu.VMEM((2, 18, ny, nz), F32),
            pltpu.VMEM((window + 1, 9, ny, nz), F32),
            pltpu.VMEM((3 * window * half, 4 * nz), BF16),
            pltpu.VMEM((3 * window * half, 4 * nz), BF16),
            pltpu.VMEM((half * (stride + 1), 2 * NCZ), F32),
        ],
        name="elements",
        compiler_params=pltpu.CompilerParams(vmem_limit_bytes=24 * MIB),
        cost_estimate=pl.CostEstimate(flops=10**10, bytes_accessed=10 * MIB, transcendentals=0),
    )(span_x, coef, displacement, adjoint, *halos, linear, net, y_back, z_back)


def on_device(sizes, offsets, displacement, adjoint, span_x, span_y, span_z):
    nodes_x, nodes_y, nodes_z = span_x.shape[0], span_y.shape[0], span_z.shape[0]
    nx, _, ny, nz = shape = displacement.shape
    swap = [(0, 1), (1, 0)]

    xf = shifted(jnp.concatenate([displacement[0], adjoint[0]], axis=0), LENGTH, sizes)
    y_face, z_face, *tables = brick_tables(displacement, adjoint, span_x, span_y, span_z)
    yf = shifted(call(widen_kernel, array(nx + 1, 8, nz), y_face, xf), WIDTH, sizes)
    net = brick_net(shape, offsets, span_x, *tables[4:])
    zf = shifted(call(deepen_kernel, array(6, ny + 8, nz), z_face, xf, yf), DEPTH, sizes)
    keep, send = brick_terms(span_x, tables, net, displacement, adjoint, (xf, yf, zf))

    size_l, size_w, size_d = sizes[LENGTH], sizes[WIDTH], sizes[DEPTH]
    size_x, size_zl = size_w // 2, 2
    lanes = 2 * NCZ
    stride = keep.shape[0] // (size_x * size_d)
    size_y = size_l // size_zl
    blocks, part = size_zl * size_d, 3 * NCX // size_l
    terms = keep + lax.ppermute(send, "c", swap)
    terms = lax.all_to_all(terms.reshape(size_x, size_d * stride, lanes), "x", 0, 0, tiled=True)
    rows = part * size_y
    terms = call(
        spread_kernel,
        array(blocks, rows + 8, lanes),
        span_x,
        terms.reshape(size_x, size_d, stride, lanes),
        scratch=[((3 * NCX, lanes), F32)],
    )
    terms = lax.all_to_all(terms, ("zl", "zh"), 0, 0, tiled=True)
    terms = call(collect_kernel, array(size_y, rows + 8, lanes), terms)
    terms = lax.all_to_all(terms, "y", 0, 0, tiled=True)
    elements = (nodes_x - 1) * (nodes_y - 1) * (nodes_z - 1)
    rows = call(
        functools.partial(scale_kernel, elements), array(blocks, rows, lanes), terms
    )
    rows = lax.all_to_all(rows, ("zl", "zh"), 0, 0, tiled=True)
    rows = call(
        repack_kernel,
        array(size_x, 3 * size_d, NCX, lanes),
        rows,
        scratch=[((NCX, lanes), F32)],
    )
    rows = lax.all_to_all(rows, "x", 0, 0, tiled=True)
    other = lax.ppermute(rows, "c", swap)
    return call(place_kernel, array(3, NCX, NCY * NCZ), rows, other)


def solution(mesh):
    count_x, count_y, count_z = mesh.devices.shape
    fine = Mesh(
        mesh.devices.reshape(2, count_x // 2, count_y // 2, 2, count_z), ("zl", "y", "x", "c", "zh")
    )
    sizes = {LENGTH: count_x, WIDTH: count_y, DEPTH: count_z}
    brick = P(LENGTH, None, WIDTH, DEPTH)
    return jax.shard_map(
        functools.partial(on_device, sizes),
        mesh=fine,
        in_specs=(P(), brick, brick, P(), P(), P()),
        out_specs=P(),
        check_vma=False,
    )
```

```python
import functools

import jax
import jax.numpy as jnp
from jax import lax
from jax.experimental import pallas as pl
from jax.experimental.pallas import tpu as pltpu
from jax.sharding import Mesh
from jax.sharding import PartitionSpec as P

NCX = 48
NCY = 64
NCZ = 64
MU_SHEAR = 40.0
LAME_RATIO = 60.0 / 40.0
TAPER_RATE = 0.8

LENGTH = ("zl", "y")
WIDTH = ("x", "c")
DEPTH = ("zh",)
F32 = jnp.float32
BF16 = jnp.bfloat16
MIB = 1 << 20
FOLD = 1
DEPTH_SIZE = 4
PITCH = NCY + 1


def spline_weights(t):
    c = 1.0 - t
    t2 = t * t
    t3 = t2 * t
    return [
        c * c * c / 6.0,
        (3.0 * t3 - 6.0 * t2 + 4.0) / 6.0,
        (-3.0 * t3 + 3.0 * t2 + 3.0 * t + 1.0) / 6.0,
        t3 / 6.0,
    ]


def node_params(span_ref, first, count):
    total = span_ref.shape[1]
    table = jnp.broadcast_to(span_ref[...].astype(F32), (count, total))
    place = lax.broadcasted_iota(jnp.int32, (count, total), 1)
    node = jnp.minimum(first + lax.broadcasted_iota(jnp.int32, (count, total), 0), total - 1)
    own = jnp.sum(jnp.where(place == node, table, 0.0), axis=1, keepdims=True)
    matches = table == own
    counted = jnp.sum(jnp.where(matches, 1.0, 0.0), axis=1, keepdims=True)
    earlier = jnp.sum(jnp.where(matches & (place < node), 1.0, 0.0), axis=1, keepdims=True)
    return own, (earlier + 0.5) / counted


def node_rows(own, t, columns):
    offset = columns - own
    out = jnp.zeros(columns.shape, F32)
    for k, weight in enumerate(spline_weights(t)):
        out = out + jnp.where(offset == float(k), weight, 0.0)
    return out


def element_rows(lower, upper, columns, live):
    low, high = node_rows(*lower, columns), node_rows(*upper, columns)
    return jnp.concatenate(
        [jnp.where(live, low + high, 0.0), jnp.where(live, high - low, 0.0)], axis=0
    )


def split(value):
    high = value.astype(BF16)
    return high, (value - high.astype(F32)).astype(BF16)


def dot(a, b):
    return lax.dot_general(a, b, (((1,), (0,)), ((), ())), preferred_element_type=F32)


def face_kernel(u_ref, w_ref, y_ref, z_ref):
    layers = u_ref.shape[0]
    rows, lanes = u_ref.shape[2], u_ref.shape[3]
    lane = lax.broadcasted_iota(jnp.int32, (rows, lanes), 1)
    for f in range(6):
        source = (u_ref, w_ref)[f // 3]
        c = f % 3
        packed = jnp.zeros((rows, lanes), F32)
        for i in range(layers):
            y_ref[i, pl.ds(f, 1)] = source[i, c, pl.ds(0, 1)]
            value = source[i, c]
            packed = jnp.where(lane == i, value if i == 0 else pltpu.roll(value, i, 1), packed)
        z_ref[f] = packed
    for i in range(layers):
        y_ref[i, pl.ds(6, 2)] = jnp.zeros((2, lanes), F32)


def widen_kernel(y_ref, xf_ref, out_ref):
    layers = y_ref.shape[0]
    out_ref[pl.ds(0, layers)] = y_ref[...]
    for f in range(6):
        out_ref[layers, pl.ds(f, 1)] = xf_ref[f, pl.ds(0, 1)]
    out_ref[layers, pl.ds(6, 2)] = jnp.zeros((2, out_ref.shape[2]), F32)


def deepen_kernel(z_ref, xf_ref, yf_ref, out_ref):
    layers = yf_ref.shape[0] - 1
    rows, lanes = z_ref.shape[1:]
    lane = lax.broadcasted_iota(jnp.int32, (rows, lanes), 1)
    edge = jnp.zeros((8, lanes), F32)
    for i in range(layers + 1):
        value = yf_ref[i]
        edge = jnp.where(lane[:8] == i, value if i == 0 else pltpu.roll(value, i, 1), edge)
    for f in range(6):
        far = pltpu.roll(xf_ref[f], layers, 1)
        out_ref[f, pl.ds(0, rows)] = jnp.where(lane == layers, far, z_ref[f])
        out_ref[f, pl.ds(rows, 8)] = jnp.broadcast_to(edge[f : f + 1], (8, lanes))


def table_kernel(
    nx, sx_ref, sy_ref, sz_ref, coef_ref, lin_ref, yb_ref, zb_ref, zf_ref, yf_ref
):
    ny, nz = lin_ref.shape[1:]
    nodes_x, nodes_y, nodes_z = sx_ref.shape[1], sy_ref.shape[1], sz_ref.shape[1]
    step_x = 2.0 * nodes_x / (NCX - 3)
    step_y = 2.0 * nodes_y / (NCY - 3)
    step_z = 2.0 * nodes_z / (NCZ - 3)
    start_x = lax.axis_index(LENGTH) * nx
    start_y = lax.axis_index(WIDTH) * ny
    start_z = lax.axis_index(DEPTH) * nz
    lanes = 2 * NCZ

    rows = coef_ref.shape[1]
    own, t = node_params(sx_ref, start_x, rows)
    own_up, t_up = node_params(sx_ref, start_x + 1, rows)
    climbs = own_up > own
    low = spline_weights(t) + [jnp.zeros_like(t)]
    high = spline_weights(t_up)
    high = [
        jnp.where(climbs, high[k - 1] if k else 0.0, high[k] if k < 4 else 0.0) for k in range(5)
    ]
    dx = (own_up - own) + (t_up - t)
    rate = TAPER_RATE / (NCX - 1)
    both = (own_up + own) + (t_up + t) + 2.0
    columns = [low[k] + high[k] for k in range(5)] + [high[k] - low[k] for k in range(5)]
    columns += [4.0 * step_x * dx, 2.0 * rate * dx, 4.0 + 2.0 * rate * both]
    for k, column in enumerate(columns):
        coef_ref[k] = jnp.broadcast_to(column, (rows, lanes))

    lower = node_params(sy_ref, start_y, ny)
    upper = node_params(sy_ref, start_y + 1, ny)
    live_y = start_y + lax.broadcasted_iota(jnp.int32, (ny, lanes), 0) < nodes_y - 1
    lane = lax.broadcasted_iota(jnp.int32, (ny, lanes), 1)
    half = NCY // 2
    y_rows = element_rows(lower, upper, (lane % NCY).astype(F32), live_y)
    for r, step in enumerate((step_x, step_y, step_z)):
        hi, lo = split(step * y_rows)
        some = jnp.concatenate([hi, lo[:, :NCY]], axis=1)
        none = jnp.zeros_like(some)
        yf_ref[r] = jnp.concatenate(
            [
                jnp.concatenate([some if g == h else none for h in range(FOLD)], axis=1)
                for g in range(FOLD)
            ],
            axis=0,
        )
    place = lane % half
    core = (lax.axis_index("c") + 2 * place // half) % 2
    owner = (place % (half // 2)) // DEPTH_SIZE * 2 + core
    paired = 2 * (owner * DEPTH_SIZE + place % DEPTH_SIZE) + (lane % NCY) // half
    y_rows = element_rows(lower, upper, paired.astype(F32), live_y)
    turned = jnp.transpose(jnp.concatenate([y_rows, y_rows], axis=0))[:NCY]
    hi, lo = split(turned)
    yb_ref[...] = jnp.concatenate([hi, lo[:, : 2 * ny]], axis=1)
    place = (upper[0] + lower[0]) + (upper[1] + lower[1]) + (2.0 - (NCY - 1))
    rise = (upper[0] - lower[0]) + (upper[1] - lower[1])
    live_z = start_z + lane < nodes_z - 1
    live = live_y & live_z
    lin_ref[0] = jnp.where(live, step_y * place, 0.0)
    lin_ref[1] = jnp.where(live, step_y * rise, 0.0)
    lin_ref[4] = jnp.where(live, 0.0, 1.0)
    lin_ref[5] = jnp.where(live, 1.0, 0.0)

    lower = node_params(sz_ref, start_z, nz)
    upper = node_params(sz_ref, start_z + 1, nz)
    live_z = start_z + lax.broadcasted_iota(jnp.int32, (nz, lanes), 0) < nodes_z - 1
    lane = lax.broadcasted_iota(jnp.int32, (nz, lanes), 1)
    z_rows = element_rows(lower, upper, (lane % NCZ).astype(F32), live_z)
    wide = lax.broadcasted_iota(jnp.int32, z_rows.shape, 1)
    hi, lo = split(
        jnp.concatenate(
            [jnp.where(wide < NCZ, z_rows, 0.0), jnp.where(wide < NCZ, 0.0, z_rows)], axis=0
        )
    )
    zb_ref[...] = jnp.concatenate([hi, lo], axis=1)
    turned = jnp.transpose(z_rows)
    tall = lax.broadcasted_iota(jnp.int32, turned.shape, 0) < NCZ
    hi, lo = split(
        jnp.concatenate([jnp.where(tall, turned, 0.0), jnp.where(tall, 0.0, turned)], axis=1)
    )
    zf_ref[...] = jnp.concatenate([hi, lo], axis=0)
    place = (upper[0] + lower[0]) + (upper[1] + lower[1]) + (2.0 - (NCZ - 1))
    rise = (upper[0] - lower[0]) + (upper[1] - lower[1])
    place = jnp.transpose(jnp.broadcast_to(step_z * place, (nz, lanes)))[:ny]
    rise = jnp.transpose(jnp.broadcast_to(step_z * rise, (nz, lanes)))[:ny]
    lin_ref[2] = jnp.where(live, place, 0.0)
    lin_ref[3] = jnp.where(live, rise, 0.0)


def net_kernel(sx_smem, o_ref, zf_ref, yf_ref, q_ref, plain_ref, slope_ref):
    window = q_ref.shape[0] - 1
    ny, nz = q_ref.shape[2:]
    lanes = 2 * NCZ
    half = NCY // 2
    start_x = lax.axis_index(LENGTH) * (window - 4)
    group = 16

    def along_z(step, carry):
        r = step // (half // group)
        pair = lax.rem(step, half // group) * group
        wide = [
            o_ref[r, :, pl.ds(pl.multiple_of((pair + g) * lanes, lanes), lanes)]
            for g in range(group)
        ]
        wide = jnp.concatenate(wide, axis=0)
        full = dot(jnp.concatenate([wide, wide], axis=1), zf_ref[...])
        for g in range(group):
            part = full[g * NCX : (g + 1) * NCX]
            for p in range(2):
                rows = pl.ds(r * NCX * PITCH + 2 * (pair + g) + p, NCX, stride=PITCH)
                plain_ref[rows] = part[:, 2 * p * nz : (2 * p + 1) * nz]
                slope_ref[rows] = part[:, (2 * p + 1) * nz : (2 * p + 2) * nz]
        return carry

    lax.fori_loop(0, 3 * half // group, along_z, 0)

    start = jnp.minimum(sx_smem[start_x], NCX - window)

    def along_y(step, carry):
        for r in range(3):
            both = []
            for g in range(FOLD):
                rows = pl.ds((r * NCX + start + step * FOLD + g) * PITCH, NCY)
                hi, lo = split(jnp.concatenate([plain_ref[rows], slope_ref[rows]], axis=1))
                both += [hi, lo, hi]
            full = dot(yf_ref[r], jnp.concatenate(both, axis=0))
            for g in range(FOLD):
                part = full[g * 2 * ny : (g + 1) * 2 * ny]
                q_ref[step * FOLD + g, 3 * r] = part[:ny, :nz]
                q_ref[step * FOLD + g, 3 * r + 1] = part[ny:, :nz]
                q_ref[step * FOLD + g, 3 * r + 2] = part[:ny, nz:]
        return carry

    lax.fori_loop(0, window // FOLD, along_y, 0, unroll=7)
    q_ref[window] = jnp.zeros(q_ref.shape[1:], F32)


def cofactors(m):
    out = [[None] * 3 for _ in range(3)]
    for r in range(3):
        r1, r2 = (r + 1) % 3, (r + 2) % 3
        for c in range(3):
            c1, c2 = (c + 1) % 3, (c + 2) % 3
            out[r][c] = m[r1][c1] * m[r2][c2] - m[r1][c2] * m[r2][c1]
    return out


def dot3(a, b):
    return a[0] * b[0] + a[1] * b[1] + a[2] * b[2]


def column(m, c):
    return [m[0][c], m[1][c], m[2][c]]


def element_gradient(jac, grad_u, grad_w, dead):
    cof = cofactors(jac)
    det = dot3(jac[0], cof[0])
    scale = 1.0 / (det + dead)
    inv_t = [[cof[r][c] * scale for c in range(3)] for r in range(3)]
    strain = [[dot3(grad_u[r], inv_t[c]) for c in range(3)] for r in range(3)]
    virt = [[dot3(grad_w[r], inv_t[c]) for c in range(3)] for r in range(3)]
    deform = [[strain[r][c] + 1.0 if r == c else strain[r][c] for c in range(3)] for r in range(3)]
    reduced = [[deform[r][c] - virt[r][c] for c in range(3)] for r in range(3)]
    cof_d = cofactors(deform)
    det_d = dot3(deform[0], cof_d[0])
    log_d = jnp.log(det_d)
    scale_d = 1.0 / det_d
    flip = [[cof_d[r][c] * scale_d for c in range(3)] for r in range(3)]
    mixed = [[dot3(column(virt, a), column(flip, b)) for b in range(3)] for a in range(3)]
    trace = mixed[0][0] + mixed[1][1] + mixed[2][2]
    factor = 1.0 - LAME_RATIO * log_d
    shift = factor + LAME_RATIO * trace
    inner = [
        [factor * mixed[a][b] + shift if a == b else factor * mixed[a][b] for b in range(3)]
        for a in range(3)
    ]
    quad = [[None] * 3 for _ in range(3)]
    for a in range(3):
        for b in range(a, 3):
            quad[a][b] = dot3(column(reduced, a), column(reduced, b)) - dot3(
                column(virt, a), column(virt, b)
            )
            quad[b][a] = quad[a][b]
    level = (
        0.5 * (quad[0][0] + quad[1][1] + quad[2][2])
        + (0.5 * LAME_RATIO * log_d - 1.0) * log_d
        - 1.5
        + factor * (1.0 + trace)
        + LAME_RATIO * trace
    )
    tensor = [
        [reduced[a][b] - quad[a][b] - dot3(flip[a], column(inner, b)) for b in range(3)]
        for a in range(3)
    ]
    for a in range(3):
        tensor[a][a] = tensor[a][a] + level
    return det, [[dot3(tensor[r], column(cof, s)) for s in range(3)] for r in range(3)]


def element_kernel(
    sx_smem, coef_ref, u_ref, w_ref, xf_ref, yf_ref, zf_ref, lin_ref, q_ref, yb_ref, zb_ref,
    keep_ref, send_ref, raw, sums, diffs, planes, acc, left_hi, left_lo, stage,
):
    layers, _, ny, nz = u_ref.shape
    window = q_ref.shape[0] - 1
    start_x = lax.axis_index(LENGTH) * layers
    live_layers = jnp.minimum(layers, sx_smem.shape[0] - 1 - start_x)
    start = jnp.minimum(sx_smem[start_x], NCX - window)
    rows = ny + 8
    lane = lax.broadcasted_iota(jnp.int32, (rows, nz), 1)

    acc[...] = jnp.zeros(acc.shape, F32)

    def make_planes(i):
        slot = lax.rem(i, 2)

        edge = yf_ref[i]
        for f in range(6):
            raw[f, pl.ds(ny, 1)] = edge[f : f + 1]

        @pl.when(i < layers)
        def _():
            for f in range(6):
                raw[f, pl.ds(0, ny)] = (u_ref, w_ref)[f // 3][i, f % 3]

        @pl.when(i >= layers)
        def _():
            for f in range(6):
                raw[f, pl.ds(0, ny)] = xf_ref[f]

        for f in range(6):
            here = raw[f]
            beyond = pltpu.roll(zf_ref[f], nz - 1 - i, 1)
            there = jnp.where(lane == nz - 1, beyond, pltpu.roll(here, nz - 1, 1))
            sums[f] = here + there
            diffs[f] = there - here
        for f in range(6):
            low, high = sums[f, pl.ds(0, ny)], sums[f, pl.ds(1, ny)]
            planes[slot, 3 * f] = low + high
            planes[slot, 3 * f + 1] = high - low
            planes[slot, 3 * f + 2] = diffs[f, pl.ds(0, ny)] + diffs[f, pl.ds(1, ny)]

    raw[:, pl.ds(ny, 8)] = jnp.zeros((6, 8, nz), F32)
    make_planes(jnp.int32(0))

    def layer(i, volume):
        make_planes(i + 1)
        new, old = lax.rem(i + 1, 2), lax.rem(i, 2)
        first = sx_smem[start_x + i] - start
        coef = [coef_ref[k, pl.ds(i, 1)] for k in range(13)]
        total, delta = coef[:5], coef[5:10]
        for block in range(ny // 16):
            at = pl.ds(16 * block, 16)
            jac = [[None] * 3 for _ in range(3)]
            for r in range(3):
                for s in range(3):
                    weight = delta if s == 0 else total
                    value = weight[0] * q_ref[first, 3 * r + s, at]
                    for k in range(1, 5):
                        value = value + weight[k] * q_ref[first + k, 3 * r + s, at]
                    jac[r][s] = value
            jac[0][0] = jac[0][0] + coef[10] * lin_ref[5, at]
            jac[1][0] = jac[1][0] + coef[11] * lin_ref[0, at]
            jac[1][1] = jac[1][1] + coef[12] * lin_ref[1, at]
            jac[2][0] = jac[2][0] + coef[11] * lin_ref[2, at]
            jac[2][2] = jac[2][2] + coef[12] * lin_ref[3, at]
            grads = []
            for f in range(6):
                grads.append(
                    [
                        planes[new, 3 * f, at] - planes[old, 3 * f, at],
                        planes[new, 3 * f + 1, at] + planes[old, 3 * f + 1, at],
                        planes[new, 3 * f + 2, at] + planes[old, 3 * f + 2, at],
                    ]
                )
            det, gradient = element_gradient(jac, grads[:3], grads[3:], lin_ref[4, at])
            volume = volume + det[:8] + det[8:]
            for r in range(3):
                for s in range(3):
                    weight = delta if s == 0 else total
                    for k in range(5):
                        p = (first + k, 3 * r + s, at)
                        acc[p] = acc[p] + weight[k] * gradient[r][s]
        return volume

    volume = lax.fori_loop(0, live_layers, layer, jnp.zeros((8, nz), F32))

    blank = jnp.zeros((ny, nz), BF16)
    half = NCY // 2

    def along_width(t, carry):
        for r in range(3):
            hi, lo = [], []
            for s in range(3):
                h, l = split(acc[t, 3 * r + s])
                hi.append(h)
                lo.append(l)
            hi = jnp.concatenate(
                [jnp.concatenate([hi[0], hi[2]], axis=1), jnp.concatenate([hi[1], blank], axis=1)],
                axis=0,
            )
            lo = jnp.concatenate(
                [jnp.concatenate([lo[0], lo[2]], axis=1), jnp.concatenate([lo[1], blank], axis=1)],
                axis=0,
            )
            full = dot(yb_ref[...], jnp.concatenate([hi, lo, hi], axis=0))
            high, low = split(full)
            at = pl.ds(pl.multiple_of((t * 3 + r) * half, half), half)
            left_hi[at, pl.ds(0, 2 * nz)] = high[:half]
            left_hi[at, pl.ds(2 * nz, 2 * nz)] = high[half:]
            left_lo[at, pl.ds(0, 2 * nz)] = low[:half]
            left_lo[at, pl.ds(2 * nz, 2 * nz)] = low[half:]
        return carry

    lax.fori_loop(0, window, along_width, 0, unroll=7)

    kept = half // 2
    rows_out = keep_ref.shape[0] // kept
    pitch = rows_out + 1
    batch = 12

    def along_depth(step, carry):
        at = pl.ds(pl.multiple_of(step * batch * half, half), batch * half)
        full = dot(left_hi[at], zb_ref[...])
        full = full[:, : 2 * NCZ] + full[:, 2 * NCZ :] + dot(left_lo[at], zb_ref[:, : 2 * NCZ])
        for b in range(batch):
            stage[pl.ds(step * batch + b, half, stride=pitch)] = full[b * half : (b + 1) * half]
        return carry

    lax.fori_loop(0, 3 * window // batch, along_depth, 0, unroll=7)

    total = jnp.sum(volume, axis=0, keepdims=True)
    spare = lax.broadcasted_iota(jnp.int32, (rows_out - 3 * window, nz), 0)
    last = jnp.where(spare == 0, jnp.broadcast_to(total, spare.shape), 0.0)
    for q in range(half):
        out_ref = keep_ref if q < kept else send_ref
        base = (q % kept) * rows_out
        out_ref[pl.ds(base, 3 * window)] = stage[pl.ds(q * pitch, 3 * window)]
        out_ref[pl.ds(base + 3 * window, rows_out - 3 * window)] = last


def spread_kernel(sx_smem, in_ref, out_ref, dense):
    parts, depth, rows, lanes = in_ref.shape
    blocks, each = out_ref.shape[0] // depth, out_ref.shape[1] - 8
    owners = lax.axis_size(LENGTH)
    nx = sx_smem.shape[0] // owners
    window = nx + 4
    start = jnp.minimum(sx_smem[lax.axis_index(LENGTH) * nx], NCX - window)
    dense[...] = jnp.zeros(dense.shape, F32)
    row = lax.broadcasted_iota(jnp.int32, (8, lanes), 0)
    for d in range(depth):
        total = in_ref[0, d]
        for p in range(1, parts):
            total = total + in_ref[p, d]
        dense[pl.ds(3 * start, 3 * window)] = total[: 3 * window]
        last = jnp.where(row == 0, total[3 * window : 3 * window + 1], 0.0)
        for block in range(blocks):
            at = block * depth + d
            out_ref[at, pl.ds(0, each)] = dense[pl.ds(block * each, each)]
            out_ref[at, pl.ds(each, 8)] = last


def collect_kernel(in_ref, out_ref):
    total = in_ref[0]
    for p in range(1, in_ref.shape[0]):
        total = total + in_ref[p]
    for p in range(out_ref.shape[0]):
        out_ref[p] = total


def scale_kernel(elements, in_ref, out_ref):
    rows = out_ref.shape[1]
    total = in_ref[0]
    for p in range(1, in_ref.shape[0]):
        total = total + in_ref[p]
    volume = jnp.sum(total[rows : rows + 1], axis=1, keepdims=True)
    total = total[:rows] * (elements * MU_SHEAR / volume)
    for p in range(out_ref.shape[0]):
        out_ref[p] = total


def repack_kernel(in_ref, out_ref, plane):
    copies, blocks, rows, lanes = out_ref.shape
    depth = blocks // 3
    parts = in_ref.shape[0] // depth
    each = rows // parts
    for r in range(3):
        for d in range(depth):
            for part in range(parts):
                plane[pl.ds(part * each, each)] = in_ref[part * depth + d, pl.ds(r, each, stride=3)]
            value = plane[...]
            for copy in range(copies):
                out_ref[copy, r * depth + d] = value


def place_kernel(own_ref, other_ref, out_ref):
    chips, blocks, rows, lanes = own_ref.shape
    depth = blocks // 3
    core = lax.axis_index("c")
    for ref, c in ((own_ref, core), (other_ref, 1 - core)):
        for x in range(chips):
            for r in range(3):
                for d in range(depth):
                    at = ((2 * x + c) * depth + d) * lanes
                    out_ref[r, :, pl.ds(pl.multiple_of(at, lanes), lanes)] = ref[x, r * depth + d]


def shifted(value, axes, sizes):
    return lax.ppermute(value, axes, [(i, i - 1) for i in range(1, sizes[axes])])


VMEM = pl.BlockSpec(memory_space=pltpu.VMEM)
SMEM = pl.BlockSpec(memory_space=pltpu.SMEM)


def call(kernel, out_shape, *operands, scratch=(), limit=16, flops=10**6):
    return pl.pallas_call(
        kernel,
        out_shape=out_shape,
        in_specs=[SMEM if o.ndim == 1 else VMEM for o in operands],
        out_specs=jax.tree.map(lambda _: VMEM, out_shape),
        scratch_shapes=[pltpu.VMEM(shape, dtype) for shape, dtype in scratch],
        name=getattr(kernel, "func", kernel).__name__.removesuffix("_kernel"),
        compiler_params=pltpu.CompilerParams(vmem_limit_bytes=limit * MIB),
        cost_estimate=pl.CostEstimate(flops=flops, bytes_accessed=MIB, transcendentals=0),
    )(*operands)


def array(*shape, dtype=F32):
    return jax.ShapeDtypeStruct(shape, dtype)


def brick_faces(displacement, adjoint):
    nx, _, ny, nz = displacement.shape
    return call(face_kernel, (array(nx, 8, nz), array(6, ny, nz)), displacement, adjoint)


def brick_tables(shape, span_x, span_y, span_z):
    nx, _, ny, nz = shape
    return call(
        functools.partial(table_kernel, nx),
        (
            array(13, -(-nx // 8) * 8, nz),
            array(6, ny, nz),
            array(NCY, 6 * ny, dtype=BF16),
            array(4 * nz, 4 * NCZ, dtype=BF16),
            array(4 * NCZ, 4 * nz, dtype=BF16),
            array(3, FOLD * 2 * ny, FOLD * 3 * NCY, dtype=BF16),
        ),
        *[s.reshape(1, s.shape[0]) for s in (span_x, span_y, span_z)],
        flops=10**7,
    )


def brick_net(shape, offsets, span_x, z_front, y_front):
    nx, _, ny, nz = shape
    return call(
        net_kernel,
        array(nx + 5, 9, ny, nz),
        span_x,
        offsets,
        z_front,
        y_front,
        scratch=[((3 * NCX * PITCH, nz), F32)] * 2,
        limit=20,
        flops=2 * 10**9,
    )


def brick_terms(span_x, tables, net, displacement, adjoint, halos):
    nx, _, ny, nz = displacement.shape
    coef, linear, y_back, z_back = tables[:4]
    window = nx + 4
    half = NCY // 2
    stride = -(-(3 * window + 1) // 8) * 8
    return pl.pallas_call(
        element_kernel,
        out_shape=(jax.ShapeDtypeStruct((half // 2 * stride, 2 * NCZ), F32),) * 2,
        in_specs=[SMEM] + [VMEM] * 10,
        out_specs=(VMEM,) * 2,
        scratch_shapes=[
            pltpu.VMEM((6, ny + 8, nz), F32),
            pltpu.VMEM((6, ny + 8, nz), F32),
            pltpu.VMEM((6, ny + 8, nz), F32),
            pltpu.VMEM((2, 18, ny, nz), F32),
            pltpu.VMEM((window + 1, 9, ny, nz), F32),
            pltpu.VMEM((3 * window * half, 4 * nz), BF16),
            pltpu.VMEM((3 * window * half, 4 * nz), BF16),
            pltpu.VMEM((half * (stride + 1), 2 * NCZ), F32),
        ],
        name="elements",
        compiler_params=pltpu.CompilerParams(vmem_limit_bytes=24 * MIB),
        cost_estimate=pl.CostEstimate(flops=10**10, bytes_accessed=10 * MIB, transcendentals=0),
    )(span_x, coef, displacement, adjoint, *halos, linear, net, y_back, z_back)


def on_device(sizes, offsets, displacement, adjoint, span_x, span_y, span_z):
    nodes_x, nodes_y, nodes_z = span_x.shape[0], span_y.shape[0], span_z.shape[0]
    nx, _, ny, nz = shape = displacement.shape
    swap = [(0, 1), (1, 0)]

    xf = shifted(jnp.concatenate([displacement[0], adjoint[0]], axis=0), LENGTH, sizes)
    y_face, z_face = brick_faces(displacement, adjoint)
    tables = brick_tables(shape, span_x, span_y, span_z)
    yf = shifted(call(widen_kernel, array(nx + 1, 8, nz), y_face, xf), WIDTH, sizes)
    net = brick_net(shape, offsets, span_x, *tables[4:])
    zf = shifted(call(deepen_kernel, array(6, ny + 8, nz), z_face, xf, yf), DEPTH, sizes)
    keep, send = brick_terms(span_x, tables, net, displacement, adjoint, (xf, yf, zf))

    size_l, size_w, size_d = sizes[LENGTH], sizes[WIDTH], sizes[DEPTH]
    size_x, size_zl = size_w // 2, 2
    lanes = 2 * NCZ
    stride = keep.shape[0] // (size_x * size_d)
    size_y = size_l // size_zl
    blocks, part = size_zl * size_d, 3 * NCX // size_l
    terms = keep + lax.ppermute(send, "c", swap)
    terms = lax.all_to_all(terms.reshape(size_x, size_d * stride, lanes), "x", 0, 0, tiled=True)
    rows = part * size_y
    terms = call(
        spread_kernel,
        array(blocks, rows + 8, lanes),
        span_x,
        terms.reshape(size_x, size_d, stride, lanes),
        scratch=[((3 * NCX, lanes), F32)],
    )
    terms = lax.all_to_all(terms, ("zl", "zh"), 0, 0, tiled=True)
    terms = call(collect_kernel, array(size_y, rows + 8, lanes), terms)
    terms = lax.all_to_all(terms, "y", 0, 0, tiled=True)
    elements = (nodes_x - 1) * (nodes_y - 1) * (nodes_z - 1)
    rows = call(
        functools.partial(scale_kernel, elements), array(blocks, rows, lanes), terms
    )
    rows = lax.all_to_all(rows, ("zl", "zh"), 0, 0, tiled=True)
    rows = call(
        repack_kernel,
        array(size_x, 3 * size_d, NCX, lanes),
        rows,
        scratch=[((NCX, lanes), F32)],
    )
    rows = lax.all_to_all(rows, "x", 0, 0, tiled=True)
    other = lax.ppermute(rows, "c", swap)
    return call(place_kernel, array(3, NCX, NCY * NCZ), rows, other)


def solution(mesh):
    count_x, count_y, count_z = mesh.devices.shape
    fine = Mesh(
        mesh.devices.reshape(2, count_x // 2, count_y // 2, 2, count_z), ("zl", "y", "x", "c", "zh")
    )
    sizes = {LENGTH: count_x, WIDTH: count_y, DEPTH: count_z}
    brick = P(LENGTH, None, WIDTH, DEPTH)
    return jax.shard_map(
        functools.partial(on_device, sizes),
        mesh=fine,
        in_specs=(P(), brick, brick, P(), P(), P()),
        out_specs=P(),
        check_vma=False,
    )
```

```python
import functools

import jax
import jax.numpy as jnp
from jax import lax
from jax.experimental import pallas as pl
from jax.experimental.pallas import tpu as pltpu
from jax.sharding import Mesh
from jax.sharding import PartitionSpec as P

NCX = 48
NCY = 64
NCZ = 64
MU_SHEAR = 40.0
LAME_RATIO = 60.0 / 40.0
TAPER_RATE = 0.8

LENGTH = ("zl", "y")
WIDTH = ("x", "c")
DEPTH = ("zh",)
F32 = jnp.float32
BF16 = jnp.bfloat16
MIB = 1 << 20
FOLD = 1
DEPTH_SIZE = 4
PITCH = NCY + 1


def spline_weights(t):
    c = 1.0 - t
    t2 = t * t
    t3 = t2 * t
    return [
        c * c * c / 6.0,
        (3.0 * t3 - 6.0 * t2 + 4.0) / 6.0,
        (-3.0 * t3 + 3.0 * t2 + 3.0 * t + 1.0) / 6.0,
        t3 / 6.0,
    ]


def node_params(span_ref, first, count):
    total = span_ref.shape[1]
    table = jnp.broadcast_to(span_ref[...].astype(F32), (count, total))
    place = lax.broadcasted_iota(jnp.int32, (count, total), 1)
    node = jnp.minimum(first + lax.broadcasted_iota(jnp.int32, (count, total), 0), total - 1)
    own = jnp.sum(jnp.where(place == node, table, 0.0), axis=1, keepdims=True)
    matches = table == own
    counted = jnp.sum(jnp.where(matches, 1.0, 0.0), axis=1, keepdims=True)
    earlier = jnp.sum(jnp.where(matches & (place < node), 1.0, 0.0), axis=1, keepdims=True)
    return own, (earlier + 0.5) / counted


def node_rows(own, t, columns):
    offset = columns - own
    out = jnp.zeros(columns.shape, F32)
    for k, weight in enumerate(spline_weights(t)):
        out = out + jnp.where(offset == float(k), weight, 0.0)
    return out


def element_rows(lower, upper, columns, live):
    low, high = node_rows(*lower, columns), node_rows(*upper, columns)
    return jnp.concatenate(
        [jnp.where(live, low + high, 0.0), jnp.where(live, high - low, 0.0)], axis=0
    )


def split(value):
    high = value.astype(BF16)
    return high, (value - high.astype(F32)).astype(BF16)


def dot(a, b):
    return lax.dot_general(a, b, (((1,), (0,)), ((), ())), preferred_element_type=F32)


def face_kernel(u_ref, w_ref, y_ref, z_ref):
    layers = u_ref.shape[0]
    rows, lanes = u_ref.shape[2], u_ref.shape[3]
    lane = lax.broadcasted_iota(jnp.int32, (rows, lanes), 1)
    for f in range(6):
        source = (u_ref, w_ref)[f // 3]
        c = f % 3
        packed = jnp.zeros((rows, lanes), F32)
        for i in range(layers):
            y_ref[i, pl.ds(f, 1)] = source[i, c, pl.ds(0, 1)]
            value = source[i, c]
            packed = jnp.where(lane == i, value if i == 0 else pltpu.roll(value, i, 1), packed)
        z_ref[f] = packed
    for i in range(layers):
        y_ref[i, pl.ds(6, 2)] = jnp.zeros((2, lanes), F32)


def widen_kernel(y_ref, xf_ref, out_ref):
    layers = y_ref.shape[0]
    out_ref[pl.ds(0, layers)] = y_ref[...]
    for f in range(6):
        out_ref[layers, pl.ds(f, 1)] = xf_ref[f, pl.ds(0, 1)]
    out_ref[layers, pl.ds(6, 2)] = jnp.zeros((2, out_ref.shape[2]), F32)


def deepen_kernel(z_ref, xf_ref, yf_ref, out_ref):
    layers = yf_ref.shape[0] - 1
    rows, lanes = z_ref.shape[1:]
    lane = lax.broadcasted_iota(jnp.int32, (rows, lanes), 1)
    edge = jnp.zeros((8, lanes), F32)
    for i in range(layers + 1):
        value = yf_ref[i]
        edge = jnp.where(lane[:8] == i, value if i == 0 else pltpu.roll(value, i, 1), edge)
    for f in range(6):
        far = pltpu.roll(xf_ref[f], layers, 1)
        out_ref[f, pl.ds(0, rows)] = jnp.where(lane == layers, far, z_ref[f])
        out_ref[f, pl.ds(rows, 8)] = jnp.broadcast_to(edge[f : f + 1], (8, lanes))


def table_kernel(
    nx, sx_ref, sy_ref, sz_ref, coef_ref, lin_ref, yb_ref, zb_ref, zf_ref, yf_ref
):
    ny, nz = lin_ref.shape[1:]
    nodes_x, nodes_y, nodes_z = sx_ref.shape[1], sy_ref.shape[1], sz_ref.shape[1]
    step_x = 2.0 * nodes_x / (NCX - 3)
    step_y = 2.0 * nodes_y / (NCY - 3)
    step_z = 2.0 * nodes_z / (NCZ - 3)
    start_x = lax.axis_index(LENGTH) * nx
    start_y = lax.axis_index(WIDTH) * ny
    start_z = lax.axis_index(DEPTH) * nz
    lanes = 2 * NCZ

    rows = coef_ref.shape[1]
    own, t = node_params(sx_ref, start_x, rows)
    own_up, t_up = node_params(sx_ref, start_x + 1, rows)
    climbs = own_up > own
    low = spline_weights(t) + [jnp.zeros_like(t)]
    high = spline_weights(t_up)
    high = [
        jnp.where(climbs, high[k - 1] if k else 0.0, high[k] if k < 4 else 0.0) for k in range(5)
    ]
    dx = (own_up - own) + (t_up - t)
    rate = TAPER_RATE / (NCX - 1)
    both = (own_up + own) + (t_up + t) + 2.0
    columns = [low[k] + high[k] for k in range(5)] + [high[k] - low[k] for k in range(5)]
    columns += [4.0 * step_x * dx, 2.0 * rate * dx, 4.0 + 2.0 * rate * both]
    for k, column in enumerate(columns):
        coef_ref[k] = jnp.broadcast_to(column, (rows, lanes))

    lower = node_params(sy_ref, start_y, ny)
    upper = node_params(sy_ref, start_y + 1, ny)
    live_y = start_y + lax.broadcasted_iota(jnp.int32, (ny, lanes), 0) < nodes_y - 1
    lane = lax.broadcasted_iota(jnp.int32, (ny, lanes), 1)
    half = NCY // 2
    y_rows = element_rows(lower, upper, (lane % NCY).astype(F32), live_y)
    for r, step in enumerate((step_x, step_y, step_z)):
        hi, lo = split(step * y_rows)
        some = jnp.concatenate([hi, lo[:, :NCY]], axis=1)
        none = jnp.zeros_like(some)
        yf_ref[r] = jnp.concatenate(
            [
                jnp.concatenate([some if g == h else none for h in range(FOLD)], axis=1)
                for g in range(FOLD)
            ],
            axis=0,
        )
    place = lane % half
    core = (lax.axis_index("c") + 2 * place // half) % 2
    owner = (place % (half // 2)) // DEPTH_SIZE * 2 + core
    paired = 2 * (owner * DEPTH_SIZE + place % DEPTH_SIZE) + (lane % NCY) // half
    y_rows = element_rows(lower, upper, paired.astype(F32), live_y)
    turned = jnp.transpose(jnp.concatenate([y_rows, y_rows], axis=0))[:NCY]
    hi, lo = split(turned)
    yb_ref[...] = jnp.concatenate([hi, lo[:, : 2 * ny]], axis=1)
    place = (upper[0] + lower[0]) + (upper[1] + lower[1]) + (2.0 - (NCY - 1))
    rise = (upper[0] - lower[0]) + (upper[1] - lower[1])
    live_z = start_z + lane < nodes_z - 1
    live = live_y & live_z
    lin_ref[0] = jnp.where(live, step_y * place, 0.0)
    lin_ref[1] = jnp.where(live, step_y * rise, 0.0)
    lin_ref[4] = jnp.where(live, 0.0, 1.0)
    lin_ref[5] = jnp.where(live, 1.0, 0.0)

    lower = node_params(sz_ref, start_z, nz)
    upper = node_params(sz_ref, start_z + 1, nz)
    live_z = start_z + lax.broadcasted_iota(jnp.int32, (nz, lanes), 0) < nodes_z - 1
    lane = lax.broadcasted_iota(jnp.int32, (nz, lanes), 1)
    z_rows = element_rows(lower, upper, (lane % NCZ).astype(F32), live_z)
    wide = lax.broadcasted_iota(jnp.int32, z_rows.shape, 1)
    hi, lo = split(
        jnp.concatenate(
            [jnp.where(wide < NCZ, z_rows, 0.0), jnp.where(wide < NCZ, 0.0, z_rows)], axis=0
        )
    )
    zb_ref[...] = jnp.concatenate([hi, lo], axis=1)
    turned = jnp.transpose(z_rows)
    tall = lax.broadcasted_iota(jnp.int32, turned.shape, 0) < NCZ
    hi, lo = split(
        jnp.concatenate([jnp.where(tall, turned, 0.0), jnp.where(tall, 0.0, turned)], axis=1)
    )
    zf_ref[...] = jnp.concatenate([hi, lo], axis=0)
    place = (upper[0] + lower[0]) + (upper[1] + lower[1]) + (2.0 - (NCZ - 1))
    rise = (upper[0] - lower[0]) + (upper[1] - lower[1])
    place = jnp.transpose(jnp.broadcast_to(step_z * place, (nz, lanes)))[:ny]
    rise = jnp.transpose(jnp.broadcast_to(step_z * rise, (nz, lanes)))[:ny]
    lin_ref[2] = jnp.where(live, place, 0.0)
    lin_ref[3] = jnp.where(live, rise, 0.0)


def net_kernel(sx_smem, o_ref, zf_ref, yf_ref, q_ref, plain_ref, slope_ref):
    window = q_ref.shape[0] - 1
    ny, nz = q_ref.shape[2:]
    lanes = 2 * NCZ
    half = NCY // 2
    start_x = lax.axis_index(LENGTH) * (window - 4)
    group = 16

    def along_z(step, carry):
        r = step // (half // group)
        pair = lax.rem(step, half // group) * group
        wide = [
            o_ref[r, :, pl.ds(pl.multiple_of((pair + g) * lanes, lanes), lanes)]
            for g in range(group)
        ]
        wide = jnp.concatenate(wide, axis=0)
        full = dot(jnp.concatenate([wide, wide], axis=1), zf_ref[...])
        for g in range(group):
            part = full[g * NCX : (g + 1) * NCX]
            for p in range(2):
                rows = pl.ds(r * NCX * PITCH + 2 * (pair + g) + p, NCX, stride=PITCH)
                plain_ref[rows] = part[:, 2 * p * nz : (2 * p + 1) * nz]
                slope_ref[rows] = part[:, (2 * p + 1) * nz : (2 * p + 2) * nz]
        return carry

    lax.fori_loop(0, 3 * half // group, along_z, 0)

    start = jnp.minimum(sx_smem[start_x], NCX - window)

    def along_y(step, carry):
        for r in range(3):
            both = []
            for g in range(FOLD):
                rows = pl.ds((r * NCX + start + step * FOLD + g) * PITCH, NCY)
                hi, lo = split(jnp.concatenate([plain_ref[rows], slope_ref[rows]], axis=1))
                both += [hi, lo, hi]
            full = dot(yf_ref[r], jnp.concatenate(both, axis=0))
            for g in range(FOLD):
                part = full[g * 2 * ny : (g + 1) * 2 * ny]
                q_ref[step * FOLD + g, 3 * r] = part[:ny, :nz]
                q_ref[step * FOLD + g, 3 * r + 1] = part[ny:, :nz]
                q_ref[step * FOLD + g, 3 * r + 2] = part[:ny, nz:]
        return carry

    lax.fori_loop(0, window // FOLD, along_y, 0, unroll=7)
    q_ref[window] = jnp.zeros(q_ref.shape[1:], F32)


def cofactors(m):
    out = [[None] * 3 for _ in range(3)]
    for r in range(3):
        r1, r2 = (r + 1) % 3, (r + 2) % 3
        for c in range(3):
            c1, c2 = (c + 1) % 3, (c + 2) % 3
            out[r][c] = m[r1][c1] * m[r2][c2] - m[r1][c2] * m[r2][c1]
    return out


def dot3(a, b):
    return a[0] * b[0] + a[1] * b[1] + a[2] * b[2]


def column(m, c):
    return [m[0][c], m[1][c], m[2][c]]


def element_gradient(jac, grad_u, grad_w, dead):
    cof = cofactors(jac)
    det = dot3(jac[0], cof[0])
    scale = 1.0 / (det + dead)
    inv_t = [[cof[r][c] * scale for c in range(3)] for r in range(3)]
    strain = [[dot3(grad_u[r], inv_t[c]) for c in range(3)] for r in range(3)]
    virt = [[dot3(grad_w[r], inv_t[c]) for c in range(3)] for r in range(3)]
    deform = [[strain[r][c] + 1.0 if r == c else strain[r][c] for c in range(3)] for r in range(3)]
    reduced = [[deform[r][c] - virt[r][c] for c in range(3)] for r in range(3)]
    cof_d = cofactors(deform)
    det_d = dot3(deform[0], cof_d[0])
    log_d = jnp.log(det_d)
    scale_d = 1.0 / det_d
    flip = [[cof_d[r][c] * scale_d for c in range(3)] for r in range(3)]
    mixed = [[dot3(column(virt, a), column(flip, b)) for b in range(3)] for a in range(3)]
    trace = mixed[0][0] + mixed[1][1] + mixed[2][2]
    factor = 1.0 - LAME_RATIO * log_d
    shift = factor + LAME_RATIO * trace
    inner = [
        [factor * mixed[a][b] + shift if a == b else factor * mixed[a][b] for b in range(3)]
        for a in range(3)
    ]
    quad = [[None] * 3 for _ in range(3)]
    for a in range(3):
        for b in range(a, 3):
            quad[a][b] = dot3(column(reduced, a), column(reduced, b)) - dot3(
                column(virt, a), column(virt, b)
            )
            quad[b][a] = quad[a][b]
    level = (
        0.5 * (quad[0][0] + quad[1][1] + quad[2][2])
        + (0.5 * LAME_RATIO * log_d - 1.0) * log_d
        - 1.5
        + factor * (1.0 + trace)
        + LAME_RATIO * trace
    )
    tensor = [
        [reduced[a][b] - quad[a][b] - dot3(flip[a], column(inner, b)) for b in range(3)]
        for a in range(3)
    ]
    for a in range(3):
        tensor[a][a] = tensor[a][a] + level
    return det, [[dot3(tensor[r], column(cof, s)) for s in range(3)] for r in range(3)]


def element_kernel(
    sx_smem, coef_ref, u_ref, w_ref, xf_ref, yf_ref, zf_ref, lin_ref, q_ref, yb_ref, zb_ref,
    keep_ref, send_ref, raw, sums, diffs, planes, acc, left_hi, left_lo, stage,
):
    layers, _, ny, nz = u_ref.shape
    window = q_ref.shape[0] - 1
    start_x = lax.axis_index(LENGTH) * layers
    live_layers = jnp.minimum(layers, sx_smem.shape[0] - 1 - start_x)
    start = jnp.minimum(sx_smem[start_x], NCX - window)
    rows = ny + 8
    lane = lax.broadcasted_iota(jnp.int32, (rows, nz), 1)

    acc[...] = jnp.zeros(acc.shape, F32)

    def make_planes(i):
        slot = lax.rem(i, 2)

        edge = yf_ref[i]
        for f in range(6):
            raw[f, pl.ds(ny, 1)] = edge[f : f + 1]

        @pl.when(i < layers)
        def _():
            for f in range(6):
                raw[f, pl.ds(0, ny)] = (u_ref, w_ref)[f // 3][i, f % 3]

        @pl.when(i >= layers)
        def _():
            for f in range(6):
                raw[f, pl.ds(0, ny)] = xf_ref[f]

        for f in range(6):
            here = raw[f]
            beyond = pltpu.roll(zf_ref[f], nz - 1 - i, 1)
            there = jnp.where(lane == nz - 1, beyond, pltpu.roll(here, nz - 1, 1))
            sums[f] = here + there
            diffs[f] = there - here
        for f in range(6):
            low, high = sums[f, pl.ds(0, ny)], sums[f, pl.ds(1, ny)]
            planes[slot, 3 * f] = low + high
            planes[slot, 3 * f + 1] = high - low
            planes[slot, 3 * f + 2] = diffs[f, pl.ds(0, ny)] + diffs[f, pl.ds(1, ny)]

    raw[:, pl.ds(ny, 8)] = jnp.zeros((6, 8, nz), F32)
    make_planes(jnp.int32(0))

    def layer(i, volume):
        make_planes(i + 1)
        new, old = lax.rem(i + 1, 2), lax.rem(i, 2)
        first = sx_smem[start_x + i] - start
        coef = [coef_ref[k, pl.ds(i, 1)] for k in range(13)]
        total, delta = coef[:5], coef[5:10]
        for block in range(ny // 16):
            at = pl.ds(16 * block, 16)
            jac = [[None] * 3 for _ in range(3)]
            for r in range(3):
                for s in range(3):
                    weight = delta if s == 0 else total
                    value = weight[0] * q_ref[first, 3 * r + s, at]
                    for k in range(1, 5):
                        value = value + weight[k] * q_ref[first + k, 3 * r + s, at]
                    jac[r][s] = value
            jac[0][0] = jac[0][0] + coef[10] * lin_ref[5, at]
            jac[1][0] = jac[1][0] + coef[11] * lin_ref[0, at]
            jac[1][1] = jac[1][1] + coef[12] * lin_ref[1, at]
            jac[2][0] = jac[2][0] + coef[11] * lin_ref[2, at]
            jac[2][2] = jac[2][2] + coef[12] * lin_ref[3, at]
            grads = []
            for f in range(6):
                grads.append(
                    [
                        planes[new, 3 * f, at] - planes[old, 3 * f, at],
                        planes[new, 3 * f + 1, at] + planes[old, 3 * f + 1, at],
                        planes[new, 3 * f + 2, at] + planes[old, 3 * f + 2, at],
                    ]
                )
            det, gradient = element_gradient(jac, grads[:3], grads[3:], lin_ref[4, at])
            volume = volume + det[:8] + det[8:]
            for r in range(3):
                for s in range(3):
                    weight = delta if s == 0 else total
                    for k in range(5):
                        p = (first + k, 3 * r + s, at)
                        acc[p] = acc[p] + weight[k] * gradient[r][s]
        return volume

    volume = lax.fori_loop(0, live_layers, layer, jnp.zeros((8, nz), F32))

    blank = jnp.zeros((ny, nz), BF16)
    half = NCY // 2

    def along_width(t, carry):
        for r in range(3):
            hi, lo = [], []
            for s in range(3):
                h, l = split(acc[t, 3 * r + s])
                hi.append(h)
                lo.append(l)
            hi = jnp.concatenate(
                [jnp.concatenate([hi[0], hi[2]], axis=1), jnp.concatenate([hi[1], blank], axis=1)],
                axis=0,
            )
            lo = jnp.concatenate(
                [jnp.concatenate([lo[0], lo[2]], axis=1), jnp.concatenate([lo[1], blank], axis=1)],
                axis=0,
            )
            full = dot(yb_ref[...], jnp.concatenate([hi, lo, hi], axis=0))
            high, low = split(full)
            at = pl.ds(pl.multiple_of((t * 3 + r) * half, half), half)
            left_hi[at, pl.ds(0, 2 * nz)] = high[:half]
            left_hi[at, pl.ds(2 * nz, 2 * nz)] = high[half:]
            left_lo[at, pl.ds(0, 2 * nz)] = low[:half]
            left_lo[at, pl.ds(2 * nz, 2 * nz)] = low[half:]
        return carry

    lax.fori_loop(0, window, along_width, 0, unroll=7)

    kept = half // 2
    rows_out = keep_ref.shape[0] // kept
    pitch = rows_out + 1
    batch = 12

    def along_depth(step, carry):
        at = pl.ds(pl.multiple_of(step * batch * half, half), batch * half)
        full = dot(left_hi[at], zb_ref[...])
        full = full[:, : 2 * NCZ] + full[:, 2 * NCZ :] + dot(left_lo[at], zb_ref[:, : 2 * NCZ])
        for b in range(batch):
            stage[pl.ds(step * batch + b, half, stride=pitch)] = full[b * half : (b + 1) * half]
        return carry

    lax.fori_loop(0, 3 * window // batch, along_depth, 0, unroll=7)

    total = jnp.sum(volume, axis=0, keepdims=True)
    spare = lax.broadcasted_iota(jnp.int32, (rows_out - 3 * window, nz), 0)
    last = jnp.where(spare == 0, jnp.broadcast_to(total, spare.shape), 0.0)
    for q in range(half):
        out_ref = keep_ref if q < kept else send_ref
        base = (q % kept) * rows_out
        out_ref[pl.ds(base, 3 * window)] = stage[pl.ds(q * pitch, 3 * window)]
        out_ref[pl.ds(base + 3 * window, rows_out - 3 * window)] = last


def spread_kernel(sx_smem, in_ref, out_ref, dense):
    parts, depth, rows, lanes = in_ref.shape
    blocks, each = out_ref.shape[0] // depth, out_ref.shape[1] - 8
    owners = lax.axis_size(LENGTH)
    nx = sx_smem.shape[0] // owners
    window = nx + 4
    start = jnp.minimum(sx_smem[lax.axis_index(LENGTH) * nx], NCX - window)
    dense[...] = jnp.zeros(dense.shape, F32)
    row = lax.broadcasted_iota(jnp.int32, (8, lanes), 0)
    for d in range(depth):
        total = in_ref[0, d]
        for p in range(1, parts):
            total = total + in_ref[p, d]
        dense[pl.ds(3 * start, 3 * window)] = total[: 3 * window]
        last = jnp.where(row == 0, total[3 * window : 3 * window + 1], 0.0)
        for block in range(blocks):
            at = block * depth + d
            out_ref[at, pl.ds(0, each)] = dense[pl.ds(block * each, each)]
            out_ref[at, pl.ds(each, 8)] = last


def collect_kernel(in_ref, out_ref):
    total = in_ref[0]
    for p in range(1, in_ref.shape[0]):
        total = total + in_ref[p]
    for p in range(out_ref.shape[0]):
        out_ref[p] = total


def scale_kernel(elements, in_ref, out_ref):
    rows = out_ref.shape[1]
    total = in_ref[0]
    for p in range(1, in_ref.shape[0]):
        total = total + in_ref[p]
    volume = jnp.sum(total[rows : rows + 1], axis=1, keepdims=True)
    total = total[:rows] * (elements * MU_SHEAR / volume)
    for p in range(out_ref.shape[0]):
        out_ref[p] = total


def repack_kernel(in_ref, out_ref, plane):
    copies, blocks, rows, lanes = out_ref.shape
    depth = blocks // 3
    parts = in_ref.shape[0] // depth
    each = rows // parts
    for r in range(3):
        for d in range(depth):
            for part in range(parts):
                plane[pl.ds(part * each, each)] = in_ref[part * depth + d, pl.ds(r, each, stride=3)]
            value = plane[...]
            for copy in range(copies):
                out_ref[copy, r * depth + d] = value


def place_kernel(own_ref, other_ref, out_ref):
    chips, blocks, rows, lanes = own_ref.shape
    depth = blocks // 3
    core = lax.axis_index("c")
    for ref, c in ((own_ref, core), (other_ref, 1 - core)):
        for x in range(chips):
            for r in range(3):
                for d in range(depth):
                    at = ((2 * x + c) * depth + d) * lanes
                    out_ref[r, :, pl.ds(pl.multiple_of(at, lanes), lanes)] = ref[x, r * depth + d]


def shifted(value, axes, sizes):
    return lax.ppermute(value, axes, [(i, i - 1) for i in range(1, sizes[axes])])


VMEM = pl.BlockSpec(memory_space=pltpu.VMEM)
SMEM = pl.BlockSpec(memory_space=pltpu.SMEM)


def call(kernel, out_shape, *operands, scratch=(), limit=16, flops=10**6):
    return pl.pallas_call(
        kernel,
        out_shape=out_shape,
        in_specs=[SMEM if o.ndim == 1 else VMEM for o in operands],
        out_specs=jax.tree.map(lambda _: VMEM, out_shape),
        scratch_shapes=[pltpu.VMEM(shape, dtype) for shape, dtype in scratch],
        name=getattr(kernel, "func", kernel).__name__.removesuffix("_kernel"),
        compiler_params=pltpu.CompilerParams(vmem_limit_bytes=limit * MIB),
        cost_estimate=pl.CostEstimate(flops=flops, bytes_accessed=MIB, transcendentals=0),
    )(*operands)


def array(*shape, dtype=F32):
    return jax.ShapeDtypeStruct(shape, dtype)


def brick_faces(displacement, adjoint):
    nx, _, ny, nz = displacement.shape
    return call(face_kernel, (array(nx, 8, nz), array(6, ny, nz)), displacement, adjoint)


def brick_tables(shape, span_x, span_y, span_z):
    nx, _, ny, nz = shape
    return call(
        functools.partial(table_kernel, nx),
        (
            array(13, -(-nx // 8) * 8 + 8, nz),
            array(6, ny, nz),
            array(NCY, 6 * ny, dtype=BF16),
            array(4 * nz, 4 * NCZ, dtype=BF16),
            array(4 * NCZ, 4 * nz, dtype=BF16),
            array(3, FOLD * 2 * ny, FOLD * 3 * NCY, dtype=BF16),
        ),
        *[s.reshape(1, s.shape[0]) for s in (span_x, span_y, span_z)],
        flops=10**7,
    )


def brick_net(shape, offsets, span_x, z_front, y_front):
    nx, _, ny, nz = shape
    return call(
        net_kernel,
        array(nx + 5, 9, ny, nz),
        span_x,
        offsets,
        z_front,
        y_front,
        scratch=[((3 * NCX * PITCH + 2 * NCY, nz), F32)] * 2,
        limit=20,
        flops=2 * 10**9,
    )


def brick_terms(span_x, tables, net, displacement, adjoint, halos):
    nx, _, ny, nz = displacement.shape
    coef, linear, y_back, z_back = tables[:4]
    window = nx + 4
    half = NCY // 2
    stride = -(-(3 * window + 1) // 8) * 8
    return pl.pallas_call(
        element_kernel,
        out_shape=(jax.ShapeDtypeStruct((half // 2 * stride, 2 * NCZ), F32),) * 2,
        in_specs=[SMEM] + [VMEM] * 10,
        out_specs=(VMEM,) * 2,
        scratch_shapes=[
            pltpu.VMEM((6, ny + 8, nz), F32),
            pltpu.VMEM((6, ny + 8, nz), F32),
            pltpu.VMEM((6, ny + 8, nz), F32),
            pltpu.VMEM((2, 18, ny, nz), F32),
            pltpu.VMEM((window + 1, 9, ny, nz), F32),
            pltpu.VMEM((3 * window * half, 4 * nz), BF16),
            pltpu.VMEM((3 * window * half, 4 * nz), BF16),
            pltpu.VMEM(((half + 1) * (stride + 1), 2 * NCZ), F32),
        ],
        name="elements",
        compiler_params=pltpu.CompilerParams(vmem_limit_bytes=24 * MIB),
        cost_estimate=pl.CostEstimate(flops=10**10, bytes_accessed=10 * MIB, transcendentals=0),
    )(span_x, coef, displacement, adjoint, *halos, linear, net, y_back, z_back)


def on_device(sizes, offsets, displacement, adjoint, span_x, span_y, span_z):
    nodes_x, nodes_y, nodes_z = span_x.shape[0], span_y.shape[0], span_z.shape[0]
    nx, _, ny, nz = shape = displacement.shape
    swap = [(0, 1), (1, 0)]

    xf = shifted(jnp.concatenate([displacement[0], adjoint[0]], axis=0), LENGTH, sizes)
    y_face, z_face = brick_faces(displacement, adjoint)
    tables = brick_tables(shape, span_x, span_y, span_z)
    yf = shifted(call(widen_kernel, array(nx + 1, 8, nz), y_face, xf), WIDTH, sizes)
    net = brick_net(shape, offsets, span_x, *tables[4:])
    zf = shifted(call(deepen_kernel, array(6, ny + 8, nz), z_face, xf, yf), DEPTH, sizes)
    keep, send = brick_terms(span_x, tables, net, displacement, adjoint, (xf, yf, zf))

    size_l, size_w, size_d = sizes[LENGTH], sizes[WIDTH], sizes[DEPTH]
    size_x, size_zl = size_w // 2, 2
    lanes = 2 * NCZ
    stride = keep.shape[0] // (size_x * size_d)
    size_y = size_l // size_zl
    blocks, part = size_zl * size_d, 3 * NCX // size_l
    terms = keep + lax.ppermute(send, "c", swap)
    terms = lax.all_to_all(terms.reshape(size_x, size_d * stride, lanes), "x", 0, 0, tiled=True)
    rows = part * size_y
    terms = call(
        spread_kernel,
        array(blocks, rows + 8, lanes),
        span_x,
        terms.reshape(size_x, size_d, stride, lanes),
        scratch=[((3 * NCX + 8, lanes), F32)],
    )
    terms = lax.all_to_all(terms, ("zl", "zh"), 0, 0, tiled=True)
    terms = call(collect_kernel, array(size_y, rows + 8, lanes), terms)
    terms = lax.all_to_all(terms, "y", 0, 0, tiled=True)
    elements = (nodes_x - 1) * (nodes_y - 1) * (nodes_z - 1)
    rows = call(
        functools.partial(scale_kernel, elements), array(blocks, rows, lanes), terms
    )
    rows = lax.all_to_all(rows, ("zl", "zh"), 0, 0, tiled=True)
    rows = call(
        repack_kernel,
        array(size_x, 3 * size_d, NCX, lanes),
        rows,
        scratch=[((NCX, lanes), F32)],
    )
    rows = lax.all_to_all(rows, "x", 0, 0, tiled=True)
    other = lax.ppermute(rows, "c", swap)
    return call(place_kernel, array(3, NCX, NCY * NCZ), rows, other)


def solution(mesh):
    count_x, count_y, count_z = mesh.devices.shape
    fine = Mesh(
        mesh.devices.reshape(2, count_x // 2, count_y // 2, 2, count_z), ("zl", "y", "x", "c", "zh")
    )
    sizes = {LENGTH: count_x, WIDTH: count_y, DEPTH: count_z}
    brick = P(LENGTH, None, WIDTH, DEPTH)
    return jax.shard_map(
        functools.partial(on_device, sizes),
        mesh=fine,
        in_specs=(P(), brick, brick, P(), P(), P()),
        out_specs=P(),
        check_vma=False,
    )
```

```python
import functools

import jax
import jax.numpy as jnp
from jax import lax
from jax.experimental import pallas as pl
from jax.experimental.pallas import tpu as pltpu
from jax.sharding import Mesh
from jax.sharding import PartitionSpec as P

NCX = 48
NCY = 64
NCZ = 64
MU_SHEAR = 40.0
LAME_RATIO = 60.0 / 40.0
TAPER_RATE = 0.8

LENGTH = ("zl", "y")
WIDTH = ("x", "c")
DEPTH = ("zh",)
F32 = jnp.float32
BF16 = jnp.bfloat16
MIB = 1 << 20
FOLD = 1
DEPTH_SIZE = 4
PITCH = NCY + 1


def spline_weights(t):
    c = 1.0 - t
    t2 = t * t
    t3 = t2 * t
    return [
        c * c * c / 6.0,
        (3.0 * t3 - 6.0 * t2 + 4.0) / 6.0,
        (-3.0 * t3 + 3.0 * t2 + 3.0 * t + 1.0) / 6.0,
        t3 / 6.0,
    ]


def node_params(span_ref, first, count):
    total = span_ref.shape[1]
    table = jnp.broadcast_to(span_ref[...].astype(F32), (count, total))
    place = lax.broadcasted_iota(jnp.int32, (count, total), 1)
    node = jnp.minimum(first + lax.broadcasted_iota(jnp.int32, (count, total), 0), total - 1)
    own = jnp.sum(jnp.where(place == node, table, 0.0), axis=1, keepdims=True)
    matches = table == own
    counted = jnp.sum(jnp.where(matches, 1.0, 0.0), axis=1, keepdims=True)
    earlier = jnp.sum(jnp.where(matches & (place < node), 1.0, 0.0), axis=1, keepdims=True)
    return own, (earlier + 0.5) / counted


def node_rows(own, t, columns):
    offset = columns - own
    out = jnp.zeros(columns.shape, F32)
    for k, weight in enumerate(spline_weights(t)):
        out = out + jnp.where(offset == float(k), weight, 0.0)
    return out


def element_rows(lower, upper, columns, live):
    low, high = node_rows(*lower, columns), node_rows(*upper, columns)
    return jnp.concatenate(
        [jnp.where(live, low + high, 0.0), jnp.where(live, high - low, 0.0)], axis=0
    )


def split(value):
    high = value.astype(BF16)
    return high, (value - high.astype(F32)).astype(BF16)


def dot(a, b):
    return lax.dot_general(a, b, (((1,), (0,)), ((), ())), preferred_element_type=F32)


def face_kernel(u_ref, w_ref, y_ref, z_ref):
    layers = u_ref.shape[0]
    rows, lanes = u_ref.shape[2], u_ref.shape[3]
    lane = lax.broadcasted_iota(jnp.int32, (rows, lanes), 1)
    for f in range(6):
        source = (u_ref, w_ref)[f // 3]
        c = f % 3
        packed = jnp.zeros((rows, lanes), F32)
        for i in range(layers):
            y_ref[i, pl.ds(f, 1)] = source[i, c, pl.ds(0, 1)]
            value = source[i, c]
            packed = jnp.where(lane == i, value if i == 0 else pltpu.roll(value, i, 1), packed)
        z_ref[f] = packed
    for i in range(layers):
        y_ref[i, pl.ds(6, 2)] = jnp.zeros((2, lanes), F32)


def widen_kernel(y_ref, xf_ref, out_ref):
    layers = y_ref.shape[0]
    out_ref[pl.ds(0, layers)] = y_ref[...]
    for f in range(6):
        out_ref[layers, pl.ds(f, 1)] = xf_ref[f, pl.ds(0, 1)]
    out_ref[layers, pl.ds(6, 2)] = jnp.zeros((2, out_ref.shape[2]), F32)


def deepen_kernel(z_ref, xf_ref, yf_ref, out_ref):
    layers = yf_ref.shape[0] - 1
    rows, lanes = z_ref.shape[1:]
    lane = lax.broadcasted_iota(jnp.int32, (rows, lanes), 1)
    edge = jnp.zeros((8, lanes), F32)
    for i in range(layers + 1):
        value = yf_ref[i]
        edge = jnp.where(lane[:8] == i, value if i == 0 else pltpu.roll(value, i, 1), edge)
    for f in range(6):
        far = pltpu.roll(xf_ref[f], layers, 1)
        out_ref[f, pl.ds(0, rows)] = jnp.where(lane == layers, far, z_ref[f])
        out_ref[f, pl.ds(rows, 8)] = jnp.broadcast_to(edge[f : f + 1], (8, lanes))


def table_kernel(
    nx, sx_ref, sy_ref, sz_ref, coef_ref, lin_ref, yb_ref, zb_ref, zf_ref, yf_ref
):
    ny, nz = lin_ref.shape[1:]
    nodes_x, nodes_y, nodes_z = sx_ref.shape[1], sy_ref.shape[1], sz_ref.shape[1]
    step_x = 2.0 * nodes_x / (NCX - 3)
    step_y = 2.0 * nodes_y / (NCY - 3)
    step_z = 2.0 * nodes_z / (NCZ - 3)
    start_x = lax.axis_index(LENGTH) * nx
    start_y = lax.axis_index(WIDTH) * ny
    start_z = lax.axis_index(DEPTH) * nz
    lanes = 2 * NCZ

    rows = coef_ref.shape[1]
    own, t = node_params(sx_ref, start_x, rows)
    own_up, t_up = node_params(sx_ref, start_x + 1, rows)
    climbs = own_up > own
    low = spline_weights(t) + [jnp.zeros_like(t)]
    high = spline_weights(t_up)
    high = [
        jnp.where(climbs, high[k - 1] if k else 0.0, high[k] if k < 4 else 0.0) for k in range(5)
    ]
    dx = (own_up - own) + (t_up - t)
    rate = TAPER_RATE / (NCX - 1)
    both = (own_up + own) + (t_up + t) + 2.0
    columns = [low[k] + high[k] for k in range(5)] + [high[k] - low[k] for k in range(5)]
    columns += [4.0 * step_x * dx, 2.0 * rate * dx, 4.0 + 2.0 * rate * both]
    for k, column in enumerate(columns):
        coef_ref[k] = jnp.broadcast_to(column, (rows, lanes))

    lower = node_params(sy_ref, start_y, ny)
    upper = node_params(sy_ref, start_y + 1, ny)
    live_y = start_y + lax.broadcasted_iota(jnp.int32, (ny, lanes), 0) < nodes_y - 1
    lane = lax.broadcasted_iota(jnp.int32, (ny, lanes), 1)
    half = NCY // 2
    y_rows = element_rows(lower, upper, (lane % NCY).astype(F32), live_y)
    for r, step in enumerate((step_x, step_y, step_z)):
        hi, lo = split(step * y_rows)
        some = jnp.concatenate([hi, lo[:, :NCY]], axis=1)
        none = jnp.zeros_like(some)
        yf_ref[r] = jnp.concatenate(
            [
                jnp.concatenate([some if g == h else none for h in range(FOLD)], axis=1)
                for g in range(FOLD)
            ],
            axis=0,
        )
    place = lane % half
    core = (lax.axis_index("c") + 2 * place // half) % 2
    owner = (place % (half // 2)) // DEPTH_SIZE * 2 + core
    paired = 2 * (owner * DEPTH_SIZE + place % DEPTH_SIZE) + (lane % NCY) // half
    y_rows = element_rows(lower, upper, paired.astype(F32), live_y)
    turned = jnp.transpose(jnp.concatenate([y_rows, y_rows], axis=0))[:NCY]
    hi, lo = split(turned)
    yb_ref[...] = jnp.concatenate([hi, lo[:, : 2 * ny]], axis=1)
    place = (upper[0] + lower[0]) + (upper[1] + lower[1]) + (2.0 - (NCY - 1))
    rise = (upper[0] - lower[0]) + (upper[1] - lower[1])
    live_z = start_z + lane < nodes_z - 1
    live = live_y & live_z
    lin_ref[0] = jnp.where(live, step_y * place, 0.0)
    lin_ref[1] = jnp.where(live, step_y * rise, 0.0)
    lin_ref[4] = jnp.where(live, 0.0, 1.0)
    lin_ref[5] = jnp.where(live, 1.0, 0.0)

    lower = node_params(sz_ref, start_z, nz)
    upper = node_params(sz_ref, start_z + 1, nz)
    live_z = start_z + lax.broadcasted_iota(jnp.int32, (nz, lanes), 0) < nodes_z - 1
    lane = lax.broadcasted_iota(jnp.int32, (nz, lanes), 1)
    z_rows = element_rows(lower, upper, (lane % NCZ).astype(F32), live_z)
    wide = lax.broadcasted_iota(jnp.int32, z_rows.shape, 1)
    hi, lo = split(
        jnp.concatenate(
            [jnp.where(wide < NCZ, z_rows, 0.0), jnp.where(wide < NCZ, 0.0, z_rows)], axis=0
        )
    )
    zb_ref[...] = jnp.concatenate([hi, lo], axis=1)
    turned = jnp.transpose(z_rows)
    tall = lax.broadcasted_iota(jnp.int32, turned.shape, 0) < NCZ
    hi, lo = split(
        jnp.concatenate([jnp.where(tall, turned, 0.0), jnp.where(tall, 0.0, turned)], axis=1)
    )
    zf_ref[...] = jnp.concatenate([hi, lo], axis=0)
    place = (upper[0] + lower[0]) + (upper[1] + lower[1]) + (2.0 - (NCZ - 1))
    rise = (upper[0] - lower[0]) + (upper[1] - lower[1])
    place = jnp.transpose(jnp.broadcast_to(step_z * place, (nz, lanes)))[:ny]
    rise = jnp.transpose(jnp.broadcast_to(step_z * rise, (nz, lanes)))[:ny]
    lin_ref[2] = jnp.where(live, place, 0.0)
    lin_ref[3] = jnp.where(live, rise, 0.0)


def net_kernel(sx_smem, o_ref, zf_ref, yf_ref, q_ref, plain_ref, slope_ref):
    window = q_ref.shape[0] - 1
    ny, nz = q_ref.shape[2:]
    lanes = 2 * NCZ
    half = NCY // 2
    start_x = lax.axis_index(LENGTH) * (window - 4)
    group = 16

    def along_z(step, carry):
        r = step // (half // group)
        pair = lax.rem(step, half // group) * group
        wide = [
            o_ref[r, :, pl.ds(pl.multiple_of((pair + g) * lanes, lanes), lanes)]
            for g in range(group)
        ]
        wide = jnp.concatenate(wide, axis=0)
        full = dot(jnp.concatenate([wide, wide], axis=1), zf_ref[...])
        for g in range(group):
            part = full[g * NCX : (g + 1) * NCX]
            for p in range(2):
                rows = pl.ds(r * NCX * PITCH + 2 * (pair + g) + p, NCX, stride=PITCH)
                plain_ref[rows] = part[:, 2 * p * nz : (2 * p + 1) * nz]
                slope_ref[rows] = part[:, (2 * p + 1) * nz : (2 * p + 2) * nz]
        return carry

    lax.fori_loop(0, 3 * half // group, along_z, 0)

    start = jnp.minimum(sx_smem[start_x], NCX - window)

    def along_y(step, carry):
        for r in range(3):
            both = []
            for g in range(FOLD):
                rows = pl.ds((r * NCX + start + step * FOLD + g) * PITCH, NCY)
                hi, lo = split(jnp.concatenate([plain_ref[rows], slope_ref[rows]], axis=1))
                both += [hi, lo, hi]
            full = dot(yf_ref[r], jnp.concatenate(both, axis=0))
            for g in range(FOLD):
                part = full[g * 2 * ny : (g + 1) * 2 * ny]
                q_ref[step * FOLD + g, 3 * r] = part[:ny, :nz]
                q_ref[step * FOLD + g, 3 * r + 1] = part[ny:, :nz]
                q_ref[step * FOLD + g, 3 * r + 2] = part[:ny, nz:]
        return carry

    lax.fori_loop(0, window // FOLD, along_y, 0, unroll=7)
    q_ref[window] = jnp.zeros(q_ref.shape[1:], F32)


def cofactors(m):
    out = [[None] * 3 for _ in range(3)]
    for r in range(3):
        r1, r2 = (r + 1) % 3, (r + 2) % 3
        for c in range(3):
            c1, c2 = (c + 1) % 3, (c + 2) % 3
            out[r][c] = m[r1][c1] * m[r2][c2] - m[r1][c2] * m[r2][c1]
    return out


def dot3(a, b):
    return a[0] * b[0] + a[1] * b[1] + a[2] * b[2]


def column(m, c):
    return [m[0][c], m[1][c], m[2][c]]


def element_gradient(jac, grad_u, grad_w, dead):
    cof = cofactors(jac)
    det = dot3(jac[0], cof[0])
    scale = 1.0 / (det + dead)
    inv_t = [[cof[r][c] * scale for c in range(3)] for r in range(3)]
    strain = [[dot3(grad_u[r], inv_t[c]) for c in range(3)] for r in range(3)]
    virt = [[dot3(grad_w[r], inv_t[c]) for c in range(3)] for r in range(3)]
    deform = [[strain[r][c] + 1.0 if r == c else strain[r][c] for c in range(3)] for r in range(3)]
    reduced = [[deform[r][c] - virt[r][c] for c in range(3)] for r in range(3)]
    cof_d = cofactors(deform)
    det_d = dot3(deform[0], cof_d[0])
    log_d = jnp.log(det_d)
    scale_d = 1.0 / det_d
    flip = [[cof_d[r][c] * scale_d for c in range(3)] for r in range(3)]
    mixed = [[dot3(column(virt, a), column(flip, b)) for b in range(3)] for a in range(3)]
    trace = mixed[0][0] + mixed[1][1] + mixed[2][2]
    factor = 1.0 - LAME_RATIO * log_d
    shift = factor + LAME_RATIO * trace
    inner = [
        [factor * mixed[a][b] + shift if a == b else factor * mixed[a][b] for b in range(3)]
        for a in range(3)
    ]
    quad = [[None] * 3 for _ in range(3)]
    for a in range(3):
        for b in range(a, 3):
            quad[a][b] = dot3(column(reduced, a), column(reduced, b)) - dot3(
                column(virt, a), column(virt, b)
            )
            quad[b][a] = quad[a][b]
    level = (
        0.5 * (quad[0][0] + quad[1][1] + quad[2][2])
        + (0.5 * LAME_RATIO * log_d - 1.0) * log_d
        - 1.5
        + factor * (1.0 + trace)
        + LAME_RATIO * trace
    )
    tensor = [
        [reduced[a][b] - quad[a][b] - dot3(flip[a], column(inner, b)) for b in range(3)]
        for a in range(3)
    ]
    for a in range(3):
        tensor[a][a] = tensor[a][a] + level
    return det, [[dot3(tensor[r], column(cof, s)) for s in range(3)] for r in range(3)]


def element_kernel(
    sx_smem, coef_ref, u_ref, w_ref, xf_ref, yf_ref, zf_ref, lin_ref, q_ref, yb_ref, zb_ref,
    keep_ref, send_ref, raw, sums, diffs, planes, acc, left_hi, left_lo, stage,
):
    layers, _, ny, nz = u_ref.shape
    window = q_ref.shape[0] - 1
    start_x = lax.axis_index(LENGTH) * layers
    live_layers = jnp.minimum(layers, sx_smem.shape[0] - 1 - start_x)
    start = jnp.minimum(sx_smem[start_x], NCX - window)
    rows = ny + 8
    lane = lax.broadcasted_iota(jnp.int32, (rows, nz), 1)

    acc[...] = jnp.zeros(acc.shape, F32)

    def make_planes(i):
        slot = lax.rem(i, 2)

        edge = yf_ref[i]
        for f in range(6):
            raw[f, pl.ds(ny, 1)] = edge[f : f + 1]

        @pl.when(i < layers)
        def _():
            for f in range(6):
                raw[f, pl.ds(0, ny)] = (u_ref, w_ref)[f // 3][i, f % 3]

        @pl.when(i >= layers)
        def _():
            for f in range(6):
                raw[f, pl.ds(0, ny)] = xf_ref[f]

        for f in range(6):
            here = raw[f]
            beyond = pltpu.roll(zf_ref[f], nz - 1 - i, 1)
            there = jnp.where(lane == nz - 1, beyond, pltpu.roll(here, nz - 1, 1))
            sums[f] = here + there
            diffs[f] = there - here
        for f in range(6):
            low, high = sums[f, pl.ds(0, ny)], sums[f, pl.ds(1, ny)]
            planes[slot, 3 * f] = low + high
            planes[slot, 3 * f + 1] = high - low
            planes[slot, 3 * f + 2] = diffs[f, pl.ds(0, ny)] + diffs[f, pl.ds(1, ny)]

    raw[:, pl.ds(ny, 8)] = jnp.zeros((6, 8, nz), F32)
    make_planes(jnp.int32(0))

    def layer(i, volume):
        make_planes(i + 1)
        new, old = lax.rem(i + 1, 2), lax.rem(i, 2)
        first = sx_smem[start_x + i] - start
        coef = [coef_ref[k, pl.ds(i, 1)] for k in range(13)]
        total, delta = coef[:5], coef[5:10]
        for block in range(ny // 16):
            at = pl.ds(16 * block, 16)
            jac = [[None] * 3 for _ in range(3)]
            for r in range(3):
                for s in range(3):
                    weight = delta if s == 0 else total
                    value = weight[0] * q_ref[first, 3 * r + s, at]
                    for k in range(1, 5):
                        value = value + weight[k] * q_ref[first + k, 3 * r + s, at]
                    jac[r][s] = value
            jac[0][0] = jac[0][0] + coef[10] * lin_ref[5, at]
            jac[1][0] = jac[1][0] + coef[11] * lin_ref[0, at]
            jac[1][1] = jac[1][1] + coef[12] * lin_ref[1, at]
            jac[2][0] = jac[2][0] + coef[11] * lin_ref[2, at]
            jac[2][2] = jac[2][2] + coef[12] * lin_ref[3, at]
            grads = []
            for f in range(6):
                grads.append(
                    [
                        planes[new, 3 * f, at] - planes[old, 3 * f, at],
                        planes[new, 3 * f + 1, at] + planes[old, 3 * f + 1, at],
                        planes[new, 3 * f + 2, at] + planes[old, 3 * f + 2, at],
                    ]
                )
            det, gradient = element_gradient(jac, grads[:3], grads[3:], lin_ref[4, at])
            volume = volume + det[:8] + det[8:]
            for r in range(3):
                for s in range(3):
                    weight = delta if s == 0 else total
                    for k in range(5):
                        p = (first + k, 3 * r + s, at)
                        acc[p] = acc[p] + weight[k] * gradient[r][s]
        return volume

    volume = lax.fori_loop(0, live_layers, layer, jnp.zeros((8, nz), F32))

    blank = jnp.zeros((ny, nz), BF16)
    half = NCY // 2

    def along_width(t, carry):
        for r in range(3):
            hi, lo = [], []
            for s in range(3):
                h, l = split(acc[t, 3 * r + s])
                hi.append(h)
                lo.append(l)
            hi = jnp.concatenate(
                [jnp.concatenate([hi[0], hi[2]], axis=1), jnp.concatenate([hi[1], blank], axis=1)],
                axis=0,
            )
            lo = jnp.concatenate(
                [jnp.concatenate([lo[0], lo[2]], axis=1), jnp.concatenate([lo[1], blank], axis=1)],
                axis=0,
            )
            full = dot(yb_ref[...], jnp.concatenate([hi, lo, hi], axis=0))
            high, low = split(full)
            at = pl.ds(pl.multiple_of((t * 3 + r) * half, half), half)
            left_hi[at, pl.ds(0, 2 * nz)] = high[:half]
            left_hi[at, pl.ds(2 * nz, 2 * nz)] = high[half:]
            left_lo[at, pl.ds(0, 2 * nz)] = low[:half]
            left_lo[at, pl.ds(2 * nz, 2 * nz)] = low[half:]
        return carry

    lax.fori_loop(0, window, along_width, 0, unroll=7)

    kept = half // 2
    rows_out = keep_ref.shape[0] // kept
    pitch = rows_out + 1
    batch = 12

    def along_depth(step, carry):
        at = pl.ds(pl.multiple_of(step * batch * half, half), batch * half)
        full = dot(left_hi[at], zb_ref[...])
        full = full[:, : 2 * NCZ] + full[:, 2 * NCZ :] + dot(left_lo[at], zb_ref[:, : 2 * NCZ])
        for b in range(batch):
            stage[pl.ds(step * batch + b, half, stride=pitch)] = full[b * half : (b + 1) * half]
        return carry

    lax.fori_loop(0, 3 * window // batch, along_depth, 0, unroll=7)

    total = jnp.sum(volume, axis=0, keepdims=True)
    spare = lax.broadcasted_iota(jnp.int32, (rows_out - 3 * window, nz), 0)
    last = jnp.where(spare == 0, jnp.broadcast_to(total, spare.shape), 0.0)
    for q in range(half):
        out_ref = keep_ref if q < kept else send_ref
        base = (q % kept) * rows_out
        out_ref[pl.ds(base, 3 * window)] = stage[pl.ds(q * pitch, 3 * window)]
        out_ref[pl.ds(base + 3 * window, rows_out - 3 * window)] = last


def spread_kernel(sx_smem, in_ref, out_ref, dense):
    parts, depth, rows, lanes = in_ref.shape
    blocks, each = out_ref.shape[0] // depth, out_ref.shape[1] - 8
    owners = lax.axis_size(LENGTH)
    nx = sx_smem.shape[0] // owners
    window = nx + 4
    start = jnp.minimum(sx_smem[lax.axis_index(LENGTH) * nx], NCX - window)
    dense[...] = jnp.zeros(dense.shape, F32)
    row = lax.broadcasted_iota(jnp.int32, (8, lanes), 0)
    for d in range(depth):
        total = in_ref[0, d]
        for p in range(1, parts):
            total = total + in_ref[p, d]
        dense[pl.ds(3 * start, 3 * window)] = total[: 3 * window]
        last = jnp.where(row == 0, total[3 * window : 3 * window + 1], 0.0)
        for block in range(blocks):
            at = block * depth + d
            out_ref[at, pl.ds(0, each)] = dense[pl.ds(block * each, each)]
            out_ref[at, pl.ds(each, 8)] = last


def collect_kernel(in_ref, out_ref):
    total = in_ref[0]
    for p in range(1, in_ref.shape[0]):
        total = total + in_ref[p]
    for p in range(out_ref.shape[0]):
        out_ref[p] = total


def scale_kernel(elements, in_ref, out_ref):
    rows = out_ref.shape[1]
    total = in_ref[0]
    for p in range(1, in_ref.shape[0]):
        total = total + in_ref[p]
    volume = jnp.sum(total[rows : rows + 1], axis=1, keepdims=True)
    total = total[:rows] * (elements * MU_SHEAR / volume)
    for p in range(out_ref.shape[0]):
        out_ref[p] = total


def repack_kernel(in_ref, out_ref, plane):
    copies, blocks, rows, lanes = out_ref.shape
    depth = blocks // 3
    parts = in_ref.shape[0] // depth
    each = rows // parts
    for r in range(3):
        for d in range(depth):
            for part in range(parts):
                plane[pl.ds(part * each, each)] = in_ref[part * depth + d, pl.ds(r, each, stride=3)]
            value = plane[...]
            for copy in range(copies):
                out_ref[copy, r * depth + d] = value


def place_kernel(own_ref, other_ref, out_hbm, result, sems):
    chips, blocks, rows, lanes = own_ref.shape
    depth = blocks // 3
    core = lax.axis_index("c")
    copies = []
    for r in range(3):
        for ref, c in ((own_ref, core), (other_ref, 1 - core)):
            for x in range(chips):
                for d in range(depth):
                    at = pl.multiple_of(((2 * x + c) * depth + d) * lanes, lanes)
                    result[r, :, pl.ds(at, lanes)] = ref[x, r * depth + d]
        copies.append(pltpu.make_async_copy(result.at[r], out_hbm.at[r], sems.at[r]))
        copies[-1].start()
    for copy in copies:
        copy.wait()


def shifted(value, axes, sizes):
    return lax.ppermute(value, axes, [(i, i - 1) for i in range(1, sizes[axes])])


VMEM = pl.BlockSpec(memory_space=pltpu.VMEM)
SMEM = pl.BlockSpec(memory_space=pltpu.SMEM)


def call(kernel, out_shape, *operands, scratch=(), limit=16, flops=10**6):
    return pl.pallas_call(
        kernel,
        out_shape=out_shape,
        in_specs=[SMEM if o.ndim == 1 else VMEM for o in operands],
        out_specs=jax.tree.map(lambda _: VMEM, out_shape),
        scratch_shapes=[pltpu.VMEM(shape, dtype) for shape, dtype in scratch],
        name=getattr(kernel, "func", kernel).__name__.removesuffix("_kernel"),
        compiler_params=pltpu.CompilerParams(vmem_limit_bytes=limit * MIB),
        cost_estimate=pl.CostEstimate(flops=flops, bytes_accessed=MIB, transcendentals=0),
    )(*operands)


def array(*shape, dtype=F32):
    return jax.ShapeDtypeStruct(shape, dtype)


def brick_faces(displacement, adjoint):
    nx, _, ny, nz = displacement.shape
    return call(face_kernel, (array(nx, 8, nz), array(6, ny, nz)), displacement, adjoint)


def brick_tables(shape, span_x, span_y, span_z):
    nx, _, ny, nz = shape
    return call(
        functools.partial(table_kernel, nx),
        (
            array(13, -(-nx // 8) * 8 + 8, nz),
            array(6, ny, nz),
            array(NCY, 6 * ny, dtype=BF16),
            array(4 * nz, 4 * NCZ, dtype=BF16),
            array(4 * NCZ, 4 * nz, dtype=BF16),
            array(3, FOLD * 2 * ny, FOLD * 3 * NCY, dtype=BF16),
        ),
        *[s.reshape(1, s.shape[0]) for s in (span_x, span_y, span_z)],
        flops=10**7,
    )


def brick_net(shape, offsets, span_x, z_front, y_front):
    nx, _, ny, nz = shape
    return call(
        net_kernel,
        array(nx + 5, 9, ny, nz),
        span_x,
        offsets,
        z_front,
        y_front,
        scratch=[((3 * NCX * PITCH + 2 * NCY, nz), F32)] * 2,
        limit=20,
        flops=2 * 10**9,
    )


def brick_terms(span_x, tables, net, displacement, adjoint, halos):
    nx, _, ny, nz = displacement.shape
    coef, linear, y_back, z_back = tables[:4]
    window = nx + 4
    half = NCY // 2
    stride = -(-(3 * window + 1) // 8) * 8
    return pl.pallas_call(
        element_kernel,
        out_shape=(jax.ShapeDtypeStruct((half // 2 * stride, 2 * NCZ), F32),) * 2,
        in_specs=[SMEM] + [VMEM] * 10,
        out_specs=(VMEM,) * 2,
        scratch_shapes=[
            pltpu.VMEM((6, ny + 8, nz), F32),
            pltpu.VMEM((6, ny + 8, nz), F32),
            pltpu.VMEM((6, ny + 8, nz), F32),
            pltpu.VMEM((2, 18, ny, nz), F32),
            pltpu.VMEM((window + 1, 9, ny, nz), F32),
            pltpu.VMEM((3 * window * half, 4 * nz), BF16),
            pltpu.VMEM((3 * window * half, 4 * nz), BF16),
            pltpu.VMEM(((half + 1) * (stride + 1), 2 * NCZ), F32),
        ],
        name="elements",
        compiler_params=pltpu.CompilerParams(vmem_limit_bytes=24 * MIB),
        cost_estimate=pl.CostEstimate(flops=10**10, bytes_accessed=10 * MIB, transcendentals=0),
    )(span_x, coef, displacement, adjoint, *halos, linear, net, y_back, z_back)


def on_device(sizes, offsets, displacement, adjoint, span_x, span_y, span_z):
    nodes_x, nodes_y, nodes_z = span_x.shape[0], span_y.shape[0], span_z.shape[0]
    nx, _, ny, nz = shape = displacement.shape
    swap = [(0, 1), (1, 0)]

    xf = shifted(jnp.concatenate([displacement[0], adjoint[0]], axis=0), LENGTH, sizes)
    y_face, z_face = brick_faces(displacement, adjoint)
    tables = brick_tables(shape, span_x, span_y, span_z)
    yf = shifted(call(widen_kernel, array(nx + 1, 8, nz), y_face, xf), WIDTH, sizes)
    net = brick_net(shape, offsets, span_x, *tables[4:])
    zf = shifted(call(deepen_kernel, array(6, ny + 8, nz), z_face, xf, yf), DEPTH, sizes)
    keep, send = brick_terms(span_x, tables, net, displacement, adjoint, (xf, yf, zf))

    size_l, size_w, size_d = sizes[LENGTH], sizes[WIDTH], sizes[DEPTH]
    size_x, size_zl = size_w // 2, 2
    lanes = 2 * NCZ
    stride = keep.shape[0] // (size_x * size_d)
    size_y = size_l // size_zl
    blocks, part = size_zl * size_d, 3 * NCX // size_l
    terms = keep + lax.ppermute(send, "c", swap)
    terms = lax.all_to_all(terms.reshape(size_x, size_d * stride, lanes), "x", 0, 0, tiled=True)
    rows = part * size_y
    terms = call(
        spread_kernel,
        array(blocks, rows + 8, lanes),
        span_x,
        terms.reshape(size_x, size_d, stride, lanes),
        scratch=[((3 * NCX + 8, lanes), F32)],
    )
    terms = lax.all_to_all(terms, ("zl", "zh"), 0, 0, tiled=True)
    terms = call(collect_kernel, array(size_y, rows + 8, lanes), terms)
    terms = lax.all_to_all(terms, "y", 0, 0, tiled=True)
    elements = (nodes_x - 1) * (nodes_y - 1) * (nodes_z - 1)
    rows = call(
        functools.partial(scale_kernel, elements), array(blocks, rows, lanes), terms
    )
    rows = lax.all_to_all(rows, ("zl", "zh"), 0, 0, tiled=True)
    rows = call(
        repack_kernel,
        array(size_x, 3 * size_d, NCX, lanes),
        rows,
        scratch=[((NCX, lanes), F32)],
    )
    rows = lax.all_to_all(rows, "x", 0, 0, tiled=True)
    other = lax.ppermute(rows, "c", swap)
    return pl.pallas_call(
        place_kernel,
        out_shape=array(3, NCX, NCY * NCZ),
        in_specs=[VMEM] * 2,
        out_specs=pl.BlockSpec(memory_space=pltpu.HBM),
        scratch_shapes=[
            pltpu.VMEM((3, NCX, NCY * NCZ), F32),
            pltpu.SemaphoreType.DMA((3,)),
        ],
        name="place",
        compiler_params=pltpu.CompilerParams(vmem_limit_bytes=16 * MIB),
    )(rows, other)


def solution(mesh):
    count_x, count_y, count_z = mesh.devices.shape
    fine = Mesh(
        mesh.devices.reshape(2, count_x // 2, count_y // 2, 2, count_z), ("zl", "y", "x", "c", "zh")
    )
    sizes = {LENGTH: count_x, WIDTH: count_y, DEPTH: count_z}
    brick = P(LENGTH, None, WIDTH, DEPTH)
    return jax.shard_map(
        functools.partial(on_device, sizes),
        mesh=fine,
        in_specs=(P(), brick, brick, P(), P(), P()),
        out_specs=P(),
        check_vma=False,
    )
```
